128 devices in a mesh: wide: 32 (over y, x, core), narrow: 4 (over z).
Axes of the slice: x: 4, y: 4, z: 4, core: 2. Of those that a mesh axis runs over, the one named last changes fastest.
Arguments:
- history: bfloat16 [512, 96, 768], P('wide'), may hold values from -6 to 6
- w_qkv: bfloat16 [768, 2304], replicated, may hold values from -0.21875 to 0.21875
- w_out: bfloat16 [768, 768], replicated, may hold values from -0.21875 to 0.21875
- dest_owner: int32 [512], P('wide'), may hold values from -1 to 31, as said below
- view_start: int32 [512, 4], P('wide', 'narrow'), may hold values from 0 to 32
- view_length: int32 [512, 4], P('wide', 'narrow'), may hold values from 16 to 64, as said below
- block_list: int32 [512, 4, 4, 4], P('wide', 'narrow'), may hold values from -1 to 3, as said below
- positive_offset: int32 [512, 4], P('wide', 'narrow'), may hold values from 1 to 3
Outputs:
- d_history: float32 [512, 96, 768], P('wide', 'narrow')
- d_wqkv: float32 [768, 2304], P(('wide', 'narrow'))
- d_wout: float32 [768, 768], P(('wide', 'narrow'))
The draws below stay inside these ranges and needn't reach their ends.
Inputs may be any that keep to these rules, and one draw needn't show every extreme that they name: `dest_owner`: every owner along wide encodes exactly 8 accounts; no device hands more than 1 accounts to one owner; a device holds either 16 live accounts or none. `view_length`: each account has a view of 64 events. `block_list`: the list of query block b holds b first, then distinct earlier blocks or -1.
All inputs are finite; a program needn't handle non-finite values.
Results may differ from the reference program's by a relative error of at most 0.023.
Values may be sent and summed in bfloat16 or wider, within the bound.
A program may use at most 128 MiB of HBM per device.

```python
import jax
import jax.numpy as jnp
from jax import lax

D = 768
HEAD_DIM = 64
VIEWS = 4
ACC_DEV = 8
ACCOUNT_SOURCE = 16
ACCOUNTS = 512
HIST = 96
VLEN = 64
LMIN = 16
NBV = 4
KSEL = 4
N_WIDE = 32


def draw_dest_owner(key, part):
    wide = ACCOUNTS // ACCOUNT_SOURCE
    ranking = jnp.argsort(jax.random.permutation(jax.random.fold_in(key, 11), wide)).astype(jnp.int32)
    owners = jax.random.permutation(jax.random.fold_in(key, 12), wide).astype(jnp.int32)
    subkeys = jax.random.split(jax.random.fold_in(key, 13), wide)
    shuffles = jax.vmap(lambda sub: jax.random.permutation(sub, ACCOUNT_SOURCE))(subkeys).astype(jnp.int32)
    based = 2 * ranking[:, None] + shuffles
    target = owners[based % wide]
    target = jnp.where(ranking[:, None] < wide // 2, target, -1)
    return target.reshape(ACCOUNTS).astype(jnp.int32)


def draw_view_length(key, part):
    sequence_extents = jax.random.randint(jax.random.fold_in(key, 31), (ACCOUNTS, VIEWS), LMIN, VLEN + 1)
    longest = jax.random.randint(jax.random.fold_in(key, 32), (ACCOUNTS,), 0, VIEWS)
    views = jnp.arange(VIEWS, dtype=jnp.int32)
    return jnp.where(views[None, :] == longest[:, None], VLEN, sequence_extents).astype(jnp.int32)


def draw_block_list(key, part):
    query = jnp.arange(NBV, dtype=jnp.int32)
    earlier = query[:, None] - 1 - jnp.arange(KSEL - 1, dtype=jnp.int32)[None, :]
    keep = jax.random.randint(jax.random.fold_in(key, 21), (ACCOUNTS, VIEWS, NBV, KSEL - 1), 0, 2)
    entries = jnp.where((keep > 0) & (earlier >= 0), earlier, -1)
    turn = jax.random.randint(jax.random.fold_in(key, 22), (ACCOUNTS, VIEWS, NBV, 1), 0, KSEL - 1)
    source_place = (jnp.arange(KSEL - 1, dtype=jnp.int32) - turn) % (KSEL - 1)
    rolled = jnp.take_along_axis(entries, source_place, axis=3)
    first = jnp.broadcast_to(query[:, None], (ACCOUNTS, VIEWS, NBV, 1))
    return jnp.concatenate([first, rolled], axis=3).astype(jnp.int32)


def place_ends(values, key, low, top_value):
    longest = values.shape.index(max(values.shape))
    spots = []
    for shift in (0, 1):
        where = [jax.random.randint(jax.random.fold_in(key, axis), (), 0, length) for axis, length in enumerate(values.shape)]
        where[longest] = (where[longest] + shift) % values.shape[longest]
        spots.append(tuple(where))
    return values.at[spots[0]].set(low).at[spots[1]].set(top_value)


def steps_of(own_key, extent, cuts, low, top_value):
    def one(position, blocks):
        heights = jax.random.uniform(jax.random.fold_in(jax.random.fold_in(own_key, 6), position), (blocks,), jnp.float32, low / len(cuts), top_value / len(cuts))
        return jnp.repeat(jnp.exp(heights), extent[position] // blocks).reshape((-1,) + (1,) * (len(extent) - position - 1))

    loudness = one(*cuts[0])
    for cut in cuts[1:]:
        loudness = loudness * one(*cut)
    return loudness


def normal_values(own_key, dims, scale, reach, shards=(), kind=jnp.bfloat16):
    values = jax.random.normal(own_key, dims, jnp.float32) * scale
    if len(shards) > 0:
        values = steps_of(own_key, dims, shards, -0.22, 0.18) * values
    return jnp.clip(values, min=-reach, max=reach).astype(kind)


def setup_inputs(seed: int = 0) -> dict:
    streams_of = jax.random.split(jax.random.key(seed), 9)
    return {
        "history": normal_values(streams_of[0], (ACCOUNTS, HIST, D), 1.0, 6.0, ((0, 32),)),
        "w_qkv": normal_values(streams_of[1], (D, 3 * D), D ** -0.5, 0.21875),
        "w_out": normal_values(streams_of[2], (D, D), D ** -0.5, 0.21875),
        "dest_owner": draw_dest_owner(jax.random.fold_in(streams_of[8], 71), 0),
        "view_start": place_ends(jax.random.randint(streams_of[4], (ACCOUNTS, VIEWS), 0, HIST - VLEN + 1), jax.random.fold_in(streams_of[4], 1), 0, HIST - VLEN).astype(jnp.int32),
        "view_length": draw_view_length(jax.random.fold_in(streams_of[8], 71), 0),
        "block_list": draw_block_list(jax.random.fold_in(streams_of[8], 71), 0),
        "positive_offset": place_ends(jax.random.randint(streams_of[7], (ACCOUNTS, VIEWS), 1, VIEWS), jax.random.fold_in(streams_of[7], 1), 1, VIEWS - 1).astype(jnp.int32),
    }


norm_epsilon = 1e-06
score_scale = 4.0
sharpness_divisor = 0.1
loss_scale = 512.0

def unit_heads(values):
    return values * lax.rsqrt(lax.optimization_barrier(jnp.mean(values * values, axis=-1, keepdims=True)) + norm_epsilon)

def view_forward(tokens, sequence_extents, blocks, w_qkv, w_out, displaced_query_key_value, shift_out):
    count, span, width = tokens.shape
    head_size = HEAD_DIM
    heads = width // head_size
    nblocks = blocks.shape[1]
    nlist = blocks.shape[2]
    block = span // nblocks
    rows = jnp.arange(span, dtype=jnp.int32)
    live = rows[None, :] < sequence_extents[:, None]
    tokens = jnp.where(live[:, :, None], tokens, jnp.zeros((), tokens.dtype))
    flat = tokens.reshape(count * span, width).astype(jnp.float32)
    normed = (flat * lax.rsqrt(lax.optimization_barrier(jnp.mean(flat * flat, axis=1, keepdims=True)) + norm_epsilon)).astype(jnp.bfloat16)
    mixed = jnp.dot(normed, w_qkv, preferred_element_type=jnp.float32) + displaced_query_key_value
    mixed = mixed.reshape(count, nblocks, block, 3, heads, head_size)
    query = unit_heads(mixed[:, :, :, 0]).astype(jnp.bfloat16)
    keyval = jnp.concatenate([unit_heads(mixed[:, :, :, 1:2]), mixed[:, :, :, 2:3]], axis=3).astype(jnp.bfloat16)
    safe = jnp.maximum(blocks, 0)
    picked = jax.vmap(lambda table, ids: table[ids])(keyval, safe)
    picked = picked.reshape(count, nblocks, nlist * block, 2, heads, head_size)
    keys = picked[:, :, :, 0]
    values = picked[:, :, :, 1]
    scores = jnp.einsum('cqihd,cqjhd->cqhij', query.astype(jnp.float32), keys.astype(jnp.float32)) * (score_scale / head_size)
    inner = jnp.arange(block, dtype=jnp.int32)
    qpos = jnp.arange(nblocks, dtype=jnp.int32)[:, None] * block + inner[None, :]
    kpos = (safe[:, :, :, None] * block + inner).reshape(count, nblocks, nlist * block)
    listed = jnp.broadcast_to((blocks >= 0)[:, :, :, None], (count, nblocks, nlist, block)).reshape(count, nblocks, nlist * block)
    kexp = kpos[:, :, None, :]
    qexp = qpos[None, :, :, None]
    visibility_mask = listed[:, :, None, :] & (kexp <= qexp) & ((kexp < sequence_extents[:, None, None, None]) | (kexp == qexp))
    weights = jnp.where(visibility_mask[:, :, None], jnp.exp(scores), 0.0)
    probs = (weights / lax.optimization_barrier(jnp.sum(weights, axis=-1, keepdims=True))).astype(jnp.bfloat16)
    attended = jnp.einsum('cqhij,cqjhd->cqihd', probs.astype(jnp.float32), values.astype(jnp.float32))
    attended = attended.astype(jnp.bfloat16).reshape(count * span, width)
    output = jnp.dot(attended, w_out, preferred_element_type=jnp.float32) + shift_out
    resid = flat + output
    share = jnp.where(live, 1.0, 0.0) / sequence_extents[:, None].astype(jnp.float32)
    pooled_history = lax.optimization_barrier(jnp.sum(resid.reshape(count, span, width) * share[:, :, None], axis=1))
    crop_representation = pooled_history * lax.rsqrt(lax.optimization_barrier(jnp.sum(pooled_history * pooled_history, axis=1, keepdims=True)) + norm_epsilon)
    return (crop_representation, (normed, attended))

def group_loss(crop_representation, offsets):
    total = crop_representation.shape[0]
    similarity_matrix = jnp.dot(crop_representation, crop_representation.T, precision=lax.Precision.HIGHEST) / sharpness_divisor
    index = jnp.arange(total, dtype=jnp.int32)
    positive = (index // ACC_DEV + offsets) % VIEWS * ACC_DEV + index % ACC_DEV
    weights = jnp.where(index[None, :] != index[:, None], jnp.exp(similarity_matrix), 0.0)
    chosen = lax.optimization_barrier(jnp.sum(jnp.where(index[None, :] == positive[:, None], similarity_matrix, 0.0), axis=1))
    return loss_scale * jnp.sum(jnp.log(lax.optimization_barrier(jnp.sum(weights, axis=1))) - chosen)

def reference(history, w_qkv, w_out, dest_owner, view_start, view_length, block_list, positive_offset):
    accounts, hist_len, width = history.shape
    span = VLEN
    index = jnp.arange(accounts, dtype=jnp.int32)
    keyed = jnp.where(dest_owner >= 0, dest_owner * accounts + index, N_WIDE * accounts + index)
    order = jnp.argsort(keyed)[:N_WIDE * ACC_DEV].astype(jnp.int32).reshape(N_WIDE, ACC_DEV)
    rows_total = VIEWS * ACC_DEV * span

    def contiguous_crop(source, start):
        return lax.dynamic_slice(history, (source, start, jnp.int32(0)), (1, span, width))[0]

    def one_group(carry, group_members):
        grad_qkv, grad_out = carry
        starts = view_start[group_members].T.reshape(-1)
        sequence_extents = view_length[group_members].T.reshape(-1)
        offsets = positive_offset[group_members].T.reshape(-1)
        blocks = jnp.transpose(block_list[group_members], (1, 0, 2, 3)).reshape(VIEWS * ACC_DEV, NBV, KSEL)
        sources = jnp.tile(group_members, VIEWS)
        tokens = jax.vmap(contiguous_crop)(sources, starts)

        def run(tok, displaced_query_key_value, shift_out):
            crop_representation, saved = view_forward(tok, sequence_extents, blocks, w_qkv, w_out, displaced_query_key_value, shift_out)
            return (group_loss(crop_representation, offsets), saved)
        zero_mixed = jnp.zeros((rows_total, 3 * width), jnp.float32)
        zero_out = jnp.zeros((rows_total, width), jnp.float32)
        loss, pullback, saved = jax.vjp(run, tokens, zero_mixed, zero_out, has_aux=True)
        d_tokens, g_mixed, g_out = pullback(jnp.ones((), jnp.float32))
        normed, attended = saved
        grad_qkv = grad_qkv + lax.dot_general(normed, g_mixed.astype(jnp.bfloat16), (((0,), (0,)), ((), ())), preferred_element_type=jnp.float32)
        grad_out = grad_out + lax.dot_general(attended, g_out.astype(jnp.bfloat16), (((0,), (0,)), ((), ())), preferred_element_type=jnp.float32)
        return ((grad_qkv, grad_out), (d_tokens, sources, starts))
    start_carry = (jnp.zeros((width, 3 * width), jnp.float32), jnp.zeros((width, width), jnp.float32))
    (grad_qkv, grad_out), (d_all, src_all, start_all) = lax.scan(one_group, start_carry, order)
    rows = start_all[..., None] + jnp.arange(span, dtype=jnp.int32)
    sources = jnp.broadcast_to(src_all[..., None], rows.shape)
    d_history = jnp.zeros((accounts, hist_len, width), jnp.float32).at[sources, rows].add(d_all.astype(jnp.float32))
    return (d_history, grad_qkv, grad_out)
```

```python
import functools

import jax
import jax.numpy as jnp
from jax import lax
from jax.experimental import pallas as pl
from jax.experimental.pallas import tpu as pltpu
from jax.sharding import PartitionSpec as P

BF = jnp.bfloat16
F32 = jnp.float32
I32 = jnp.int32
MESH = pl.DeviceIdType.MESH

WIDE = 32
NARROW = 4
CHIP_X = 4
CHIP_Y = 4
OWNED = 8
SLOTS = 16
D = 768
HEAD = 64
SPAN = 64
HIST = 96
GROUP = 256
ROWS = OWNED * SPAN
QROWS = HIST // 2
QCOLS = D // 2
ORROWS = HIST // NARROW
WROWS = D // WIDE
WCOLS = 4 * D
HALF = WCOLS // 2

LIVE, LEN, OFF, START, SLOT, BLOCKS = 0, 1, 2, 3, 4, 5
EPS = 1e-06
VMEM_LIMIT = 60 * 1024 * 1024


def mm(a, b):
    return jnp.dot(a, b, preferred_element_type=F32)


def mm_t(a, b):
    return lax.dot_general(a, b, (((1,), (1,)), ((), ())), preferred_element_type=F32)


def mm_l(a, b):
    return lax.dot_general(a, b, (((0,), (0,)), ((), ())), preferred_element_type=F32)


def split_hi_lo(x):
    hi = x.astype(BF)
    return hi, (x - hi.astype(F32)).astype(BF)


def iota(shape, dim):
    return lax.broadcasted_iota(I32, shape, dim)


def head_diag():
    shape = (GROUP, GROUP)
    return (iota(shape, 0) // HEAD) == (iota(shape, 1) // HEAD)


def spread_heads(x, diag):
    return jnp.where(diag, jnp.concatenate([x, x, x, x], axis=0), jnp.zeros((), x.dtype))


def gather_heads(full, diag):
    kept = jnp.where(diag, full, 0.0)
    return (kept[0:64] + kept[64:128]) + (kept[128:192] + kept[192:256])


def two_rows(x):
    hi = x.astype(BF).astype(F32)
    row = iota((8, GROUP), 0)
    return jnp.where(row == 0, hi, jnp.where(row == 1, x - hi, 0.0)).astype(BF)


def dispatch_kernel(
    msg_s, msg_v, hist, out, facts8, place, hbuf, sbuf, rbuf, frecv, fsm,
    lsem, fsem, bsend, brecv, fsend, frsem, zsend, zrecv,
):
    w = lax.axis_index("wide")
    z = lax.axis_index("narrow")
    load = pltpu.make_async_copy(
        hist.at[:, pl.ds(QROWS * (z // 2), QROWS), pl.ds(QCOLS * (z % 2), QCOLS)], hbuf, lsem
    )
    load.start()
    barrier = pltpu.get_barrier_semaphore()

    def greet(k, c):
        pl.semaphore_signal(barrier, inc=1, device_id=((w + k) % WIDE, z), device_id_type=MESH)
        return c

    lax.fori_loop(1, WIDE, greet, 0)
    for k in range(1, NARROW):
        pl.semaphore_signal(barrier, inc=1, device_id=(w, (z + k) % NARROW), device_id_type=MESH)
    pl.semaphore_wait(barrier, WIDE - 1 + NARROW - 1)

    def fact_copy(k):
        d = (w + k) % WIDE
        return pltpu.make_async_remote_copy(
            src_ref=msg_v.at[d], dst_ref=frecv.at[w], send_sem=fsend.at[k], recv_sem=frsem.at[k],
            device_id=(d, z), device_id_type=MESH,
        )

    def fact_arrival(k):
        s = (w + WIDE - k) % WIDE
        return pltpu.make_async_remote_copy(
            src_ref=msg_v.at[s], dst_ref=frecv.at[s], send_sem=fsend.at[k], recv_sem=frsem.at[k],
            device_id=(s, z), device_id_type=MESH,
        )

    def box_copy(k):
        d = (w + k) % WIDE
        return pltpu.make_async_remote_copy(
            src_ref=sbuf.at[k], dst_ref=rbuf.at[w], send_sem=bsend.at[k], recv_sem=brecv.at[k],
            device_id=(d, z), device_id_type=MESH,
        )

    def box_arrival(k):
        s = (w + WIDE - k) % WIDE
        return pltpu.make_async_remote_copy(
            src_ref=sbuf.at[k], dst_ref=rbuf.at[s], send_sem=bsend.at[k], recv_sem=brecv.at[k],
            device_id=(s, z), device_id_type=MESH,
        )

    def send_facts(k, c):
        fact_copy(k).start()
        return c

    lax.fori_loop(1, WIDE, send_facts, 0)
    load.wait()

    def send_box(k, c):
        sbuf[k] = hbuf[msg_s[(w + k) % WIDE, SLOT]]
        box_copy(k).start()
        return c

    lax.fori_loop(1, WIDE, send_box, 0)
    rbuf[w] = hbuf[msg_s[w, SLOT]]
    frecv[w] = msg_v[w]

    def wait_facts(k, c):
        fact_arrival(k).wait_recv()
        return c

    lax.fori_loop(1, WIDE, wait_facts, 0)
    down = pltpu.make_async_copy(frecv, fsm, fsem)
    down.start()
    down.wait()

    def scan(s, c):
        count, picks = c
        live = fsm[s, 0, LIVE]
        place[s] = jnp.minimum(count, OWNED - 1)
        picks = tuple(
            jnp.where((live > 0) & (count == p), s, picks[p]) for p in range(OWNED)
        )
        return count + live, picks

    _, picks = lax.fori_loop(
        0, WIDE, scan, (jnp.int32(0), tuple(jnp.int32(0) for _ in range(OWNED)))
    )
    for p in range(OWNED):
        facts8[p] = frecv[picks[p]]

    def wait_box(k, c):
        box_arrival(k).wait_recv()
        return c

    lax.fori_loop(1, WIDE, wait_box, 0)
    for p in range(OWNED):
        out[z, p] = rbuf[picks[p]]

    right = (z + 1) % NARROW
    left = (z + 3) % NARROW
    opposite = (z + 2) % NARROW
    part = OWNED // 2

    def hop(quarter, lo, size, to, n):
        where = out.at[quarter, pl.ds(lo, size)]
        return pltpu.make_async_remote_copy(
            src_ref=where, dst_ref=where, send_sem=zsend.at[n], recv_sem=zrecv.at[n],
            device_id=(w, to), device_id_type=MESH,
        )

    to_right = [hop(z, 0, part, right, 0), hop(z, part, part, right, 1)]
    to_left = [hop(z, part, part, left, 2), hop(z, 0, part, left, 3)]
    to_right[0].start()
    to_left[0].start()
    to_right[1].start()
    to_left[1].start()
    hop(left, 0, part, left, 0).wait_recv()
    on_right = hop(left, 0, part, right, 4)
    on_right.start()
    hop(right, part, part, right, 2).wait_recv()
    on_left = hop(right, part, part, left, 5)
    on_left.start()
    hop(left, part, part, left, 1).wait_recv()
    hop(right, 0, part, right, 3).wait_recv()
    hop(opposite, 0, part, left, 4).wait_recv()
    hop(opposite, part, part, right, 5).wait_recv()
    for copy in to_right + to_left + [on_right, on_left]:
        copy.wait_send()

    def drain(k, c):
        fact_copy(k).wait_send()
        box_copy(k).wait_send()
        return c

    lax.fori_loop(1, WIDE, drain, 0)


def forward_kernel(
    facts, hist, wqkv, wout, normed, qkv, inv_heads, inv_tokens, probs, pooled, mean_att
):
    diag = head_diag()
    ones = jnp.where(diag, 1.0, 0.0).astype(BF)
    row48 = iota((SPAN, QROWS), 0)
    col48 = iota((SPAN, QROWS), 1)
    for p in range(OWNED):
        start = facts[p, START]
        length = facts[p, LEN]
        rows = pl.ds(p * SPAN, SPAN)
        source = row48 + start
        alive = row48 < length
        top = jnp.where((col48 == source) & alive, 1.0, 0.0).astype(BF)
        low = jnp.where((col48 + QROWS == source) & alive, 1.0, 0.0).astype(BF)
        left = mm(top, hist[0, p]) + mm(low, hist[2, p])
        right = mm(top, hist[1, p]) + mm(low, hist[3, p])
        square = jnp.sum(left * left, axis=1, keepdims=True) + jnp.sum(
            right * right, axis=1, keepdims=True
        )
        inv = lax.rsqrt(square * (1.0 / D) + EPS)
        normed[rows, 0:QCOLS] = (left * inv).astype(BF)
        normed[rows, QCOLS:D] = (right * inv).astype(BF)
        inv_tokens[rows, :] = jnp.broadcast_to(inv, (SPAN, 128))
        scale = length.astype(F32)
        pooled[p : p + 1, 0:QCOLS] = jnp.sum(left, axis=0, keepdims=True) / scale
        pooled[p : p + 1, QCOLS:D] = jnp.sum(right, axis=0, keepdims=True) / scale
    for j in range(9):
        cols = pl.ds(j * GROUP, GROUP)
        mixed = mm(normed[...], wqkv[:, cols])
        if j < 6:
            square = mm((mixed * mixed).astype(BF), ones)
            inv = lax.rsqrt(square * (1.0 / HEAD) + EPS)
            qkv[:, cols] = (mixed * inv).astype(BF)
            inv_heads[:, cols] = inv.astype(BF)
        else:
            qkv[:, cols] = mixed.astype(BF)

    def one_view(p, c):
        rows = pl.ds(pl.multiple_of(p * SPAN, SPAN), SPAN)
        length = facts[p, LEN]
        lane = iota((16, GROUP), 1) % SPAN
        block = lane // 16
        parts = []
        for b in range(4):
            listed = block == facts[p, BLOCKS + 4 * b]
            for j in range(1, 4):
                listed = listed | (block == facts[p, BLOCKS + 4 * b + j])
            parts.append(jnp.where(listed & (lane <= iota((16, GROUP), 0) + 16 * b), 1.0, 0.0))
        allowed = jnp.concatenate(parts, axis=0)
        share = jnp.where(iota((SPAN, GROUP), 0) < length, 1.0, 0.0)
        scale = length.astype(F32)
        for g in range(3):
            cols = pl.ds(g * GROUP, GROUP)
            query = qkv[rows, cols]
            keys = spread_heads(qkv[rows, pl.ds(D + g * GROUP, GROUP)], diag)
            values = spread_heads(qkv[rows, pl.ds(2 * D + g * GROUP, GROUP)], diag)
            score = mm_t(query, keys) * (4.0 / HEAD)
            weight = jnp.exp(score) * allowed
            total = mm(weight.astype(BF), ones)
            prob = weight / total
            probs[p, :, cols] = prob.astype(BF)
            column = jnp.sum(prob * share, axis=0, keepdims=True) / scale
            got = mm(two_rows(column), values)
            mean_att[pl.ds(p, 1), cols] = got[0:1] + got[1:2]
        return c

    lax.fori_loop(0, OWNED, one_view, 0)
    hi, lo = split_hi_lo(mean_att[...])
    pooled[...] += mm(hi, wout[...]) + mm(lo, wout[...])


def loss_kernel(pooled, facts, d_pooled, mine, everyone, d_embed, send, recv):
    w = lax.axis_index("wide")
    z = lax.axis_index("narrow")
    barrier = pltpu.get_barrier_semaphore()
    for k in range(1, NARROW):
        pl.semaphore_signal(barrier, inc=1, device_id=(w, (z + k) % NARROW), device_id_type=MESH)
    pool = pooled[...]
    inv = lax.rsqrt(jnp.sum(pool * pool, axis=1, keepdims=True) + EPS)
    embed = pool * inv
    mine[:, 0:D] = embed
    mine[:, D : D + 128] = jnp.broadcast_to(facts[:, OFF : OFF + 1].astype(F32), (OWNED, 128))
    everyone[z] = mine[...]
    pl.semaphore_wait(barrier, NARROW - 1)
    copies = []
    for k in range(1, NARROW):
        copy = pltpu.make_async_remote_copy(
            src_ref=mine, dst_ref=everyone.at[z], send_sem=send.at[k], recv_sem=recv.at[k],
            device_id=(w, (z + k) % NARROW), device_id_type=MESH,
        )
        copy.start()
        copies.append(copy)
    for k in range(1, NARROW):
        s = (z + NARROW - k) % NARROW
        pltpu.make_async_remote_copy(
            src_ref=mine, dst_ref=everyone.at[s], send_sem=send.at[k], recv_sem=recv.at[k],
            device_id=(w, s), device_id_type=MESH,
        ).wait_recv()
    total = NARROW * OWNED
    full = everyone[...].reshape(total, D + 128)
    group = full[:, 0:D]
    offset = full[:, D : D + total].astype(I32)
    high = lax.Precision.HIGHEST
    logit = (
        lax.dot_general(
            group, group, (((1,), (1,)), ((), ())), precision=high, preferred_element_type=F32
        )
        / 0.1
    )
    row = iota((total, total), 0)
    col = iota((total, total), 1)
    positive = ((row // OWNED + offset) % NARROW) * OWNED + row % OWNED
    weight = jnp.where(row != col, jnp.exp(logit), 0.0)
    prob = weight / jnp.sum(weight, axis=1, keepdims=True)
    coef = (512.0 / 0.1) * (prob - jnp.where(col == positive, 1.0, 0.0))
    d_embed[...] = jnp.dot(
        coef, group, precision=high, preferred_element_type=F32
    ) + lax.dot_general(
        coef, group, (((0,), (0,)), ((), ())), precision=high, preferred_element_type=F32
    )
    own = d_embed[pl.ds(pl.multiple_of(OWNED * z, OWNED), OWNED), :]
    d_pooled[...] = inv * (own - embed * jnp.sum(own * embed, axis=1, keepdims=True))
    for copy in copies:
        copy.wait_send()


def backward_kernel(
    facts, d_pooled, mean_att, normed, qkv, inv_heads, inv_tokens, probs, wqkv, wout,
    d_hist, d_w, d_att, g_mixed, normed_t, d_normed,
):
    diag = head_diag()
    ones = jnp.where(diag, 1.0, 0.0).astype(BF)
    hi, lo = split_hi_lo(d_pooled[...])
    d_att[...] = mm_t(hi, wout[...]) + mm_t(lo, wout[...])
    att_hi, att_lo = split_hi_lo(mean_att[...])
    for j in range(3):
        cols = pl.ds(j * GROUP, GROUP)
        got = mm_l(
            jnp.concatenate([att_hi, att_lo], axis=0),
            jnp.concatenate([hi, hi], axis=0)[:, j * GROUP : (j + 1) * GROUP],
        )
        d_w[:, :, pl.ds(3 * D + j * GROUP, GROUP)] = got.reshape(WIDE, WROWS, GROUP).astype(BF)
    normed_t[...] = normed[...].T

    def one_view(p, c):
        rows = pl.ds(pl.multiple_of(p * SPAN, SPAN), SPAN)
        length = facts[p, LEN]
        share = jnp.where(iota((SPAN, GROUP), 0) < length, 1.0, 0.0)
        scale = length.astype(F32)
        for g in range(3):
            cols = pl.ds(g * GROUP, GROUP)
            kcols = pl.ds(D + g * GROUP, GROUP)
            vcols = pl.ds(2 * D + g * GROUP, GROUP)
            query = qkv[rows, cols]
            keys = spread_heads(qkv[rows, kcols], diag)
            values = spread_heads(qkv[rows, vcols], diag)
            d_row = d_att[pl.ds(p, 1), cols] / scale
            got = mm_t(two_rows(d_row), values)
            slope = got[0:1] + got[1:2]
            prob = probs[p, :, cols].astype(F32) * share
            tilted = prob * slope
            center = mm(tilted.astype(BF), ones)
            d_score = ((tilted - prob * center) * (4.0 / HEAD)).astype(BF)
            g_mixed[rows, cols] = mm(d_score, keys).astype(BF)
            g_mixed[rows, kcols] = gather_heads(mm_l(d_score, query), diag).astype(BF)
            d_rows = jnp.broadcast_to(d_row, (SPAN, GROUP)).astype(BF)
            g_mixed[rows, vcols] = gather_heads(mm_l(prob.astype(BF), d_rows), diag).astype(BF)
        return c

    lax.fori_loop(0, OWNED, one_view, 0)
    for j in range(6):
        cols = pl.ds(j * GROUP, GROUP)
        unit = qkv[:, cols].astype(F32)
        grad = g_mixed[:, cols].astype(F32)
        mean = mm((grad * unit).astype(BF), ones) * (1.0 / HEAD)
        g_mixed[:, cols] = (inv_heads[:, cols].astype(F32) * (grad - unit * mean)).astype(BF)
    for j in range(9):
        cols = pl.ds(j * GROUP, GROUP)
        got = mm(normed_t[...], g_mixed[:, cols])
        d_w[:, :, cols] = got.reshape(WIDE, WROWS, GROUP).astype(BF)
    for j in range(3):
        cols = pl.ds(j * GROUP, GROUP)
        d_normed[:, cols] = mm_t(g_mixed[...], wqkv[cols, :])
    for p in range(OWNED):
        rows = pl.ds(p * SPAN, SPAN)
        length = facts[p, LEN]
        start = facts[p, START]
        unit = normed[rows, :].astype(F32)
        grad = d_normed[rows, :]
        mean = jnp.sum(grad * unit, axis=1, keepdims=True) * (1.0 / D)
        back = inv_tokens[rows, 0:1] * (grad - unit * mean)
        back = back + d_pooled[p : p + 1, :] / length.astype(F32)
        alive = iota((SPAN, D), 0) < length
        d_tokens = jnp.where(alive, back, 0.0).astype(BF)
        put = jnp.where(iota((HIST, SPAN), 0) == iota((HIST, SPAN), 1) + start, 1.0, 0.0)
        spread = mm(put.astype(BF), d_tokens)
        for j in range(NARROW):
            d_hist[j, p] = spread[j * ORROWS : (j + 1) * ORROWS].astype(BF)


def return_kernel(
    place, dest, d_hist, d_w, out_hist, out_qkv, out_out,
    zin, dsum, sbuf, rbuf, core_in, acc, in_a, in_b, mid_a, mid_b, end_a, end_b,
    final, zbuf, zlast,
    zsend, zrecv, bsend, brecv, csem, asend, arecv, a2send, a2recv, lsend, lrecv,
):
    w = lax.axis_index("wide")
    z = lax.axis_index("narrow")
    core = w % 2
    x = (w // 2) % CHIP_X
    y = w // (2 * CHIP_X)
    barrier = pltpu.get_barrier_semaphore()

    def greet(k, c):
        pl.semaphore_signal(barrier, inc=1, device_id=((w + k) % WIDE, z), device_id_type=MESH)
        return c

    lax.fori_loop(1, WIDE, greet, 0)
    for k in range(1, NARROW):
        pl.semaphore_signal(barrier, inc=1, device_id=(w, (z + k) % NARROW), device_id_type=MESH)
    pl.semaphore_wait(barrier, WIDE - 1 + NARROW - 1)

    def remote(src, dst, send, recv, to):
        return pltpu.make_async_remote_copy(
            src_ref=src, dst_ref=dst, send_sem=send, recv_sem=recv, device_id=to,
            device_id_type=MESH,
        )

    other = w + 1 - 2 * core
    cross = remote(d_w.at[:, 1 - core], core_in, csem.at[0], csem.at[1], (other, z))
    cross.start()
    z_copies = []
    for k in range(1, NARROW):
        t = (z + k) % NARROW
        copy = remote(d_hist.at[t], zin.at[k], zsend.at[k], zrecv.at[k], (w, t))
        copy.start()
        z_copies.append(copy)
    cross.wait_recv()

    def pair(i, c):
        acc[i // CHIP_X, i % CHIP_X] = (
            d_w[i, core].astype(F32) + core_in[i].astype(F32)
        ).astype(BF)
        return c

    lax.fori_loop(0, CHIP_X * CHIP_Y, pair, 0)
    first = []
    for k in range(1, 4):
        tx = (x + k) % CHIP_X
        ty = (y + k) % CHIP_Y
        first.append(
            remote(
                acc.at[:, tx, :, pl.ds(0, HALF)], in_a.at[k], asend.at[0, k], arecv.at[0, k],
                ((y * CHIP_X + tx) * 2 + core, z),
            )
        )
        first.append(
            remote(
                acc.at[ty, :, :, pl.ds(HALF, HALF)], in_b.at[k], asend.at[1, k], arecv.at[1, k],
                ((ty * CHIP_X + x) * 2 + core, z),
            )
        )
    for copy in first:
        copy.start()

    for copy in z_copies:
        copy.wait_recv()

    def add_views(p, c):
        dsum[p] = (
            (d_hist[z, p].astype(F32) + zin[1, p].astype(F32))
            + (zin[2, p].astype(F32) + zin[3, p].astype(F32))
        ).astype(BF)
        return c

    lax.fori_loop(0, OWNED, add_views, 0)

    def box_copy(k):
        return remote(
            sbuf.at[k], rbuf.at[w], bsend.at[k], brecv.at[k], ((w + k) % WIDE, z)
        )

    def send_box(k, c):
        sbuf[k] = dsum[place[(w + k) % WIDE]]
        box_copy(k).start()
        return c

    lax.fori_loop(1, WIDE, send_box, 0)
    rbuf[w] = dsum[place[w]]

    for copy in first:
        copy.wait_recv()

    def middle(i, c):
        mid_a[i] = (
            (acc[i, x, :, 0:HALF].astype(F32) + in_a[1, i].astype(F32))
            + (in_a[2, i].astype(F32) + in_a[3, i].astype(F32))
        ).astype(BF)
        mid_b[i] = (
            (acc[y, i, :, HALF:WCOLS].astype(F32) + in_b[1, i].astype(F32))
            + (in_b[2, i].astype(F32) + in_b[3, i].astype(F32))
        ).astype(BF)
        return c

    lax.fori_loop(0, 4, middle, 0)
    second = []
    for k in range(1, 4):
        tx = (x + k) % CHIP_X
        ty = (y + k) % CHIP_Y
        second.append(
            remote(
                mid_a.at[ty], end_a.at[k], a2send.at[0, k], a2recv.at[0, k],
                ((ty * CHIP_X + x) * 2 + core, z),
            )
        )
        second.append(
            remote(
                mid_b.at[tx], end_b.at[k], a2send.at[1, k], a2recv.at[1, k],
                ((y * CHIP_X + tx) * 2 + core, z),
            )
        )
    for copy in second:
        copy.start()
    for copy in second:
        copy.wait_recv()
    final[0:WROWS, 0:HALF] = (mid_a[y].astype(F32) + end_a[1].astype(F32)) + (
        end_a[2].astype(F32) + end_a[3].astype(F32)
    )
    final[0:WROWS, HALF:WCOLS] = (mid_b[x].astype(F32) + end_b[1].astype(F32)) + (
        end_b[2].astype(F32) + end_b[3].astype(F32)
    )
    final[WROWS : WROWS + 8, :] = jnp.zeros((8, WCOLS), F32)
    for j in range(NARROW):
        zbuf[j] = final[6 * j : 6 * j + 8, :]
    last = []
    for k in range(1, NARROW):
        t = (z + k) % NARROW
        copy = remote(zbuf.at[t], zlast.at[k], lsend.at[k], lrecv.at[k], (w, t))
        copy.start()
        last.append(copy)

    def wait_box(k, c):
        s = (w + WIDE - k) % WIDE
        remote(sbuf.at[k], rbuf.at[s], bsend.at[k], brecv.at[k], (s, z)).wait_recv()
        return c

    lax.fori_loop(1, WIDE, wait_box, 0)

    def write(a, c):
        owner = dest[a]
        got = rbuf[jnp.maximum(owner, 0)].astype(F32)
        out_hist[a] = jnp.where(jnp.full((ORROWS, D), owner, I32) >= 0, got, 0.0)
        return c

    lax.fori_loop(0, SLOTS, write, 0)
    for copy in last:
        copy.wait_recv()
    total = (zbuf[z] + zlast[1]) + (zlast[2] + zlast[3])
    out_qkv[...] = total[0:6, 0 : 3 * D]
    out_out[...] = total[0:6, 3 * D : WCOLS]

    cross.wait_send()
    for copy in z_copies + first + second + last:
        copy.wait_send()

    def drain(k, c):
        box_copy(k).wait_send()
        return c

    lax.fori_loop(1, WIDE, drain, 0)


VM = pl.BlockSpec(memory_space=pltpu.VMEM)
SM = pl.BlockSpec(memory_space=pltpu.SMEM)
HB = pl.BlockSpec(memory_space=pl.ANY)
DMA = pltpu.SemaphoreType.DMA


def shape(dims, kind):
    return jax.ShapeDtypeStruct(dims, kind)


def remote_params(number):
    return pltpu.CompilerParams(
        collective_id=number, has_side_effects=True, vmem_limit_bytes=VMEM_LIMIT
    )


def dispatch(message, history):
    return pl.pallas_call(
        dispatch_kernel,
        out_shape=(
            shape((NARROW, OWNED, QROWS, QCOLS), BF),
            shape((OWNED, 1, 128), I32),
            shape((WIDE,), I32),
        ),
        in_specs=[SM, VM, HB],
        out_specs=(VM, VM, SM),
        scratch_shapes=[
            pltpu.VMEM((SLOTS, QROWS, QCOLS), BF),
            pltpu.VMEM((WIDE, QROWS, QCOLS), BF),
            pltpu.VMEM((WIDE, QROWS, QCOLS), BF),
            pltpu.VMEM((WIDE, 1, 128), I32),
            pltpu.SMEM((WIDE, 1, 128), I32),
            DMA, DMA,
            DMA((WIDE,)), DMA((WIDE,)), DMA((WIDE,)), DMA((WIDE,)),
            DMA((6,)), DMA((6,)),
        ],
        compiler_params=remote_params(0),
        name="dispatch",
    )(message, message.reshape(WIDE, 1, 128), history)


def forward(facts, hist, wqkv, wout):
    return pl.pallas_call(
        forward_kernel,
        out_shape=(
            shape((ROWS, D), BF),
            shape((ROWS, 3 * D), BF),
            shape((ROWS, 2 * D), BF),
            shape((ROWS, 128), F32),
            shape((OWNED, SPAN, D), BF),
            shape((OWNED, D), F32),
            shape((OWNED, D), F32),
        ),
        in_specs=[SM, VM, VM, VM],
        out_specs=(VM,) * 7,
        compiler_params=pltpu.CompilerParams(vmem_limit_bytes=VMEM_LIMIT),
        name="forward",
    )(facts, hist, wqkv, wout)


def loss_gradient(pooled, facts):
    return pl.pallas_call(
        loss_kernel,
        out_shape=shape((OWNED, D), F32),
        in_specs=[VM, VM],
        out_specs=VM,
        scratch_shapes=[
            pltpu.VMEM((OWNED, D + 128), F32),
            pltpu.VMEM((NARROW, OWNED, D + 128), F32),
            pltpu.VMEM((NARROW * OWNED, D), F32),
            DMA((NARROW,)), DMA((NARROW,)),
        ],
        compiler_params=remote_params(1),
        name="loss",
    )(pooled, facts)


def backward(facts, d_pooled, mean_att, normed, qkv, inv_heads, inv_tokens, probs, wqkv, wout):
    return pl.pallas_call(
        backward_kernel,
        out_shape=(
            shape((NARROW, OWNED, ORROWS, D), BF),
            shape((WIDE, WROWS, WCOLS), BF),
        ),
        in_specs=[SM] + [VM] * 9,
        out_specs=(VM, VM),
        scratch_shapes=[
            pltpu.VMEM((OWNED, D), F32),
            pltpu.VMEM((ROWS, 3 * D), BF),
            pltpu.VMEM((D, ROWS), BF),
            pltpu.VMEM((ROWS, D), F32),
        ],
        compiler_params=pltpu.CompilerParams(vmem_limit_bytes=VMEM_LIMIT),
        name="backward",
    )(facts, d_pooled, mean_att, normed, qkv, inv_heads, inv_tokens, probs, wqkv, wout)


def send_back(place, dest, d_hist, d_w):
    return pl.pallas_call(
        return_kernel,
        out_shape=(
            shape((SLOTS, ORROWS, D), F32),
            shape((6, 3 * D), F32),
            shape((6, D), F32),
        ),
        in_specs=[SM, SM, VM, VM],
        out_specs=(VM, VM, VM),
        scratch_shapes=[
            pltpu.VMEM((NARROW, OWNED, ORROWS, D), BF),
            pltpu.VMEM((OWNED, ORROWS, D), BF),
            pltpu.VMEM((WIDE, ORROWS, D), BF),
            pltpu.VMEM((WIDE, ORROWS, D), BF),
            pltpu.VMEM((16, WROWS, WCOLS), BF),
            pltpu.VMEM((4, 4, WROWS, WCOLS), BF),
            pltpu.VMEM((4, 4, WROWS, HALF), BF),
            pltpu.VMEM((4, 4, WROWS, HALF), BF),
            pltpu.VMEM((4, WROWS, HALF), BF),
            pltpu.VMEM((4, WROWS, HALF), BF),
            pltpu.VMEM((4, WROWS, HALF), BF),
            pltpu.VMEM((4, WROWS, HALF), BF),
            pltpu.VMEM((WROWS + 8, WCOLS), F32),
            pltpu.VMEM((NARROW, 8, WCOLS), F32),
            pltpu.VMEM((NARROW, 8, WCOLS), F32),
            DMA((NARROW,)), DMA((NARROW,)),
            DMA((WIDE,)), DMA((WIDE,)),
            DMA((2,)),
            DMA((2, 4)), DMA((2, 4)),
            DMA((2, 4)), DMA((2, 4)),
            DMA((NARROW,)), DMA((NARROW,)),
        ],
        compiler_params=remote_params(2),
        name="send_back",
    )(place, dest, d_hist, d_w.reshape(16, 2, WROWS, WCOLS))


def on_device(
    history, w_qkv, w_out, dest_owner, view_start, view_length, block_list, positive_offset
):
    order = jnp.arange(SLOTS, dtype=I32)
    facts = jnp.concatenate(
        [
            jnp.ones((SLOTS, 1), I32),
            view_length,
            positive_offset,
            view_start,
            order[:, None],
            block_list.reshape(SLOTS, 16),
            jnp.zeros((SLOTS, 128 - 21), I32),
        ],
        axis=1,
    )
    to = dest_owner[None, :] == jnp.arange(WIDE, dtype=I32)[:, None]
    message = jnp.sum(jnp.where(to[:, :, None], facts[None], 0), axis=1, dtype=I32)
    hist, facts8, place = dispatch(message, history)
    facts8 = facts8.reshape(OWNED, 128)
    normed, qkv, inv_heads, inv_tokens, probs, pooled, mean_att = forward(
        facts8, hist, w_qkv, w_out
    )
    d_pooled = loss_gradient(pooled, facts8)
    d_hist, d_w = backward(
        facts8, d_pooled, mean_att, normed, qkv, inv_heads, inv_tokens, probs, w_qkv, w_out
    )
    return send_back(place, dest_owner, d_hist, d_w)


def solution(mesh):
    return jax.shard_map(
        on_device,
        mesh=mesh,
        in_specs=(
            P("wide", None, None),
            P(),
            P(),
            P("wide"),
            P("wide", "narrow"),
            P("wide", "narrow"),
            P("wide", "narrow", None, None),
            P("wide", "narrow"),
        ),
        out_specs=(
            P("wide", "narrow", None),
            P(("wide", "narrow"), None),
            P(("wide", "narrow"), None),
        ),
        check_vma=False,
    )
```

```python
import jax
import jax.numpy as jnp
from jax import lax
from jax.experimental import pallas as pl
from jax.experimental.pallas import tpu as pltpu
from jax.sharding import PartitionSpec as P

BF = jnp.bfloat16
F32 = jnp.float32
I32 = jnp.int32
MESH = pl.DeviceIdType.MESH

WIDE = 32
NARROW = 4
CHIP_X = 4
CHIP_Y = 4
OWNED = 8
SLOTS = 16
D = 768
HEAD = 64
SPAN = 64
HIST = 96
GROUP = 256
ROWS = OWNED * SPAN
QROWS = HIST // 2
QCOLS = D // 2
ORROWS = HIST // NARROW
WROWS = D // WIDE
WCOLS = 4 * D
HALF = WCOLS // 2

LIVE, LEN, OFF, START, BLOCKS = 0, 1, 2, 3, 8
CHUNKS = 3
CROWS = QROWS // CHUNKS
PEERS = WIDE - 1
EPS = 1e-06
VMEM_LIMIT = 60 * 1024 * 1024


def mm(a, b):
    return jnp.dot(a, b, preferred_element_type=F32)


def mm_t(a, b):
    return lax.dot_general(a, b, (((1,), (1,)), ((), ())), preferred_element_type=F32)


def mm_l(a, b):
    return lax.dot_general(a, b, (((0,), (0,)), ((), ())), preferred_element_type=F32)


def split_hi_lo(x):
    hi = x.astype(BF)
    return hi, (x - hi.astype(F32)).astype(BF)


def iota(shape, dim):
    return lax.broadcasted_iota(I32, shape, dim)


def head_diag():
    shape = (GROUP, GROUP)
    return (iota(shape, 0) // HEAD) == (iota(shape, 1) // HEAD)


def spread_heads(x, diag):
    return jnp.where(diag, jnp.concatenate([x, x, x, x], axis=0), jnp.zeros((), x.dtype))


def gather_heads(full, diag):
    kept = jnp.where(diag, full, 0.0)
    return (kept[0:64] + kept[64:128]) + (kept[128:192] + kept[192:256])


def two_rows(x):
    hi = x.astype(BF).astype(F32)
    row = iota((8, GROUP), 0)
    return jnp.where(row == 0, hi, jnp.where(row == 1, x - hi, 0.0)).astype(BF)


def whole_kernel(
    dest, starts, lengths, offsets, lists, hist, wqkv_hbm, wout_hbm,
    out_hist, out_w,
    wqkv, wout, fact_t, fact, slot_s, message, frecv, fsm, pick_s, place_s, facts8,
    hbuf, sbuf, rbuf_0, rbuf_1, rbuf_2, crop,
    normed, normed_t, qkv, inv_heads, inv_tokens, probs, pooled, mean_att,
    mine, everyone, d_embed, d_pooled, d_att, g_mixed, d_normed, d_tokens,
    dw_a, dw_b, core_a, core_b, acc_a, acc_b, in_a, in_b, mid_a, mid_b, end_a, end_b,
    final, zbuf, zlast,
    d_hist, zhop, zcomb, zfin, dsum, sback, rback_0, rback_1, rback_2,
    wsem, lsem, fsem, factsem, boxsend, boxrecv, zsend, zrecv, esend, erecv,
    csend, crecv, asend, arecv, a2send, a2recv, lsend, lrecv,
    hsend, hrecv, backsend, backrecv,
):
    w = lax.axis_index("wide")
    z = lax.axis_index("narrow")
    core = w % 2
    x = (w // 2) % CHIP_X
    y = w // (2 * CHIP_X)
    right = (z + 1) % NARROW
    left = (z + 3) % NARROW
    opposite = (z + 2) % NARROW

    def remote(src, dst, send, recv, to):
        return pltpu.make_async_remote_copy(
            src_ref=src, dst_ref=dst, send_sem=send, recv_sem=recv, device_id=to,
            device_id_type=MESH,
        )

    rbuf = (rbuf_0, rbuf_1, rbuf_2)
    rback = (rback_0, rback_1, rback_2)

    load = pltpu.make_async_copy(
        hist.at[:, pl.ds(QROWS * (z // 2), QROWS), pl.ds(QCOLS * (z % 2), QCOLS)], hbuf, lsem
    )
    load.start()
    barrier = pltpu.get_barrier_semaphore()

    def greet(k, c):
        pl.semaphore_signal(barrier, inc=1, device_id=((w + k) % WIDE, z), device_id_type=MESH)
        return c

    lax.fori_loop(1, WIDE, greet, 0)
    for k in range(1, NARROW):
        pl.semaphore_signal(barrier, inc=1, device_id=(w, (z + k) % NARROW), device_id_type=MESH)
    load_qkv = pltpu.make_async_copy(wqkv_hbm, wqkv, wsem.at[0])
    load_out = pltpu.make_async_copy(wout_hbm, wout, wsem.at[1])
    load_qkv.start()
    load_out.start()

    fact_t[...] = jnp.zeros((128, 128), I32)
    fact_t[LIVE : LIVE + 1, :] = jnp.ones((1, 128), I32)
    fact_t[LEN : LEN + 1, 0:SLOTS] = lengths[...]
    fact_t[OFF : OFF + 1, 0:SLOTS] = offsets[...]
    fact_t[START : START + 1, 0:SLOTS] = starts[...]
    fact_t[BLOCKS : BLOCKS + 16, 0:SLOTS] = lists[...]
    fact[...] = fact_t[...].T
    owners = [dest[a] for a in range(SLOTS)]

    def find(d, c):
        slot = jnp.int32(0)
        live = jnp.int32(0)
        for a in range(SLOTS):
            hit = owners[a] == d
            slot = jnp.where(hit, a, slot)
            live = jnp.where(hit, 1, live)
        slot_s[d] = slot
        message[d] = fact[pl.ds(slot, 1), :] * live
        return c

    lax.fori_loop(0, WIDE, find, 0)
    pl.semaphore_wait(barrier, PEERS + NARROW - 1)

    def send_facts(k, c):
        d = (w + k) % WIDE
        remote(message.at[d], frecv.at[w], factsem.at[0], factsem.at[1], (d, z)).start()
        return c

    lax.fori_loop(1, WIDE, send_facts, 0)
    load.wait()
    for c in range(CHUNKS):

        def send_box(k, carry):
            d = (w + k) % WIDE
            sbuf[c, k] = hbuf[slot_s[d], CROWS * c : CROWS * (c + 1), :]
            remote(sbuf.at[c, k], rbuf[c].at[w], boxsend.at[c], boxrecv.at[c], (d, z)).start()
            return carry

        lax.fori_loop(1, WIDE, send_box, 0)
    frecv[w] = message[w]
    for c in range(CHUNKS):
        rbuf[c][w] = hbuf[slot_s[w], CROWS * c : CROWS * (c + 1), :]
    all_facts = remote(
        message.at[pl.ds(0, PEERS)], frecv.at[pl.ds(0, PEERS)], factsem.at[0], factsem.at[1],
        ((w + 1) % WIDE, z),
    )
    all_facts.wait_recv()
    down = pltpu.make_async_copy(frecv, fsm, fsem)
    down.start()
    down.wait()

    def scan(s, carry):
        count, picks = carry
        live = fsm[s, 0, LIVE]
        place_s[s] = jnp.minimum(count, OWNED - 1)
        picks = tuple(jnp.where((live > 0) & (count == p), s, picks[p]) for p in range(OWNED))
        return count + live, picks

    _, picks = lax.fori_loop(
        0, WIDE, scan, (jnp.int32(0), tuple(jnp.int32(0) for _ in range(OWNED)))
    )
    for p in range(OWNED):
        pick_s[p] = picks[p]
        facts8[p : p + 1, :] = frecv[picks[p]]

    def known(p, which):
        return fsm[pick_s[p], 0, which]

    part = OWNED // 2

    def hop(c, quarter, lo, size, to, n):
        where = crop.at[quarter, pl.ds(lo, size), pl.ds(CROWS * c, CROWS), :]
        return remote(where, where, zsend.at[c, n], zrecv.at[c, n], (w, to))

    z_sent = []

    def forward_hops(c):
        hop(c, left, 0, OWNED, left, 0).wait_recv()
        on_right = hop(c, left, 0, part, right, 2)
        on_right.start()
        hop(c, right, 0, OWNED, right, 1).wait_recv()
        on_left = hop(c, right, part, part, left, 3)
        on_left.start()
        z_sent.extend([on_right, on_left])

    all_boxes = []
    for c in range(CHUNKS):
        boxes = remote(
            sbuf.at[c, pl.ds(0, PEERS)], rbuf[c].at[pl.ds(0, PEERS)], boxsend.at[c],
            boxrecv.at[c], ((w + 1) % WIDE, z),
        )
        all_boxes.append(boxes)
        boxes.wait_recv()
        for p in range(OWNED):
            crop[z, p, CROWS * c : CROWS * (c + 1), :] = rbuf[c][picks[p]]
        to_right = hop(c, z, 0, OWNED, right, 0)
        to_left = hop(c, z, 0, OWNED, left, 1)
        to_right.start()
        to_left.start()
        z_sent.extend([to_right, to_left])
        if c > 0:
            forward_hops(c - 1)
    forward_hops(CHUNKS - 1)
    for c in range(CHUNKS):
        hop(c, opposite, 0, part, left, 2).wait_recv()
        hop(c, opposite, part, part, right, 3).wait_recv()

    diag = head_diag()
    ones = jnp.where(diag, 1.0, 0.0).astype(BF)
    row48 = iota((SPAN, QROWS), 0)
    col48 = iota((SPAN, QROWS), 1)
    for p in range(OWNED):
        start = known(p, START)
        length = known(p, LEN)
        rows = pl.ds(p * SPAN, SPAN)
        source = row48 + start
        alive = row48 < length
        top = jnp.where((col48 == source) & alive, 1.0, 0.0).astype(BF)
        low = jnp.where((col48 + QROWS == source) & alive, 1.0, 0.0).astype(BF)
        lhs = mm(top, crop[0, p]) + mm(low, crop[2, p])
        rhs = mm(top, crop[1, p]) + mm(low, crop[3, p])
        square = jnp.sum(lhs * lhs, axis=1, keepdims=True) + jnp.sum(
            rhs * rhs, axis=1, keepdims=True
        )
        inv = lax.rsqrt(square * (1.0 / D) + EPS)
        normed[rows, 0:QCOLS] = (lhs * inv).astype(BF)
        normed[rows, QCOLS:D] = (rhs * inv).astype(BF)
        inv_tokens[rows, :] = jnp.broadcast_to(inv, (SPAN, 128))
        scale = length.astype(F32)
        pooled[p : p + 1, 0:QCOLS] = jnp.sum(lhs, axis=0, keepdims=True) / scale
        pooled[p : p + 1, QCOLS:D] = jnp.sum(rhs, axis=0, keepdims=True) / scale
    load_qkv.wait()
    load_out.wait()
    for j in range(9):
        cols = pl.ds(j * GROUP, GROUP)
        mixed = mm(normed[...], wqkv[:, cols])
        if j < 6:
            square = mm((mixed * mixed).astype(BF), ones)
            inv = lax.rsqrt(square * (1.0 / HEAD) + EPS)
            qkv[:, cols] = (mixed * inv).astype(BF)
            inv_heads[:, cols] = inv.astype(BF)
        else:
            qkv[:, cols] = mixed.astype(BF)

    def attend(p, carry):
        rows = pl.ds(pl.multiple_of(p * SPAN, SPAN), SPAN)
        length = known(p, LEN)
        lane = iota((16, GROUP), 1) % SPAN
        block = lane // 16
        parts = []
        for b in range(4):
            listed = block == known(p, BLOCKS + 4 * b)
            for j in range(1, 4):
                listed = listed | (block == known(p, BLOCKS + 4 * b + j))
            parts.append(jnp.where(listed & (lane <= iota((16, GROUP), 0) + 16 * b), 1.0, 0.0))
        allowed = jnp.concatenate(parts, axis=0)
        share = jnp.where(iota((SPAN, GROUP), 0) < length, 1.0, 0.0)
        scale = length.astype(F32)
        for g in range(3):
            cols = pl.ds(g * GROUP, GROUP)
            query = qkv[rows, cols]
            keys = spread_heads(qkv[rows, pl.ds(D + g * GROUP, GROUP)], diag)
            values = spread_heads(qkv[rows, pl.ds(2 * D + g * GROUP, GROUP)], diag)
            score = mm_t(query, keys) * (4.0 / HEAD)
            weight = jnp.exp(score) * allowed
            total = mm(weight.astype(BF), ones)
            prob = weight / total
            probs[p, :, cols] = prob.astype(BF)
            column = jnp.sum(prob * share, axis=0, keepdims=True) / scale
            got = mm(two_rows(column), values)
            mean_att[pl.ds(p, 1), cols] = got[0:1] + got[1:2]
        return carry

    lax.fori_loop(0, OWNED, attend, 0)
    att_hi, att_lo = split_hi_lo(mean_att[...])
    pooled[...] += mm(att_hi, wout[...]) + mm(att_lo, wout[...])

    pool = pooled[...]
    inv_pool = lax.rsqrt(jnp.sum(pool * pool, axis=1, keepdims=True) + EPS)
    embed = pool * inv_pool
    mine[:, 0:D] = embed
    mine[:, D : D + 128] = jnp.broadcast_to(facts8[:, OFF : OFF + 1].astype(F32), (OWNED, 128))
    e_copies = []
    for k in range(1, NARROW):
        copy = remote(
            mine, everyone.at[z], esend.at[k], erecv.at[k], (w, (z + k) % NARROW)
        )
        copy.start()
        e_copies.append(copy)
    everyone[z] = mine[...]
    normed_t[...] = normed[...].T
    for k in range(1, NARROW):
        s = (z + NARROW - k) % NARROW
        remote(mine, everyone.at[s], esend.at[k], erecv.at[k], (w, s)).wait_recv()
    total = NARROW * OWNED
    full = everyone[...].reshape(total, D + 128)
    group = full[:, 0:D]
    offset = full[:, D : D + total].astype(I32)
    high = lax.Precision.HIGHEST
    logit = (
        lax.dot_general(
            group, group, (((1,), (1,)), ((), ())), precision=high, preferred_element_type=F32
        )
        / 0.1
    )
    row = iota((total, total), 0)
    col = iota((total, total), 1)
    positive = ((row // OWNED + offset) % NARROW) * OWNED + row % OWNED
    weight = jnp.where(row != col, jnp.exp(logit), 0.0)
    prob = weight / jnp.sum(weight, axis=1, keepdims=True)
    coef = (512.0 / 0.1) * (prob - jnp.where(col == positive, 1.0, 0.0))
    d_embed[...] = jnp.dot(
        coef, group, precision=high, preferred_element_type=F32
    ) + lax.dot_general(
        coef, group, (((0,), (0,)), ((), ())), precision=high, preferred_element_type=F32
    )
    own = d_embed[pl.ds(pl.multiple_of(OWNED * z, OWNED), OWNED), :]
    d_pooled[...] = inv_pool * (own - embed * jnp.sum(own * embed, axis=1, keepdims=True))

    hi, lo = split_hi_lo(d_pooled[...])
    d_att[...] = mm_t(hi, wout[...]) + mm_t(lo, wout[...])
    for j in range(3):
        got = mm_l(
            jnp.concatenate([att_hi, att_lo], axis=0),
            jnp.concatenate([hi, hi], axis=0)[:, j * GROUP : (j + 1) * GROUP],
        )
        dw_b[:, :, :, pl.ds(D + j * GROUP, GROUP)] = got.reshape(16, 2, WROWS, GROUP).astype(BF)

    def attend_back(p, carry):
        rows = pl.ds(pl.multiple_of(p * SPAN, SPAN), SPAN)
        length = known(p, LEN)
        share = jnp.where(iota((SPAN, GROUP), 0) < length, 1.0, 0.0)
        scale = length.astype(F32)
        for g in range(3):
            cols = pl.ds(g * GROUP, GROUP)
            kcols = pl.ds(D + g * GROUP, GROUP)
            vcols = pl.ds(2 * D + g * GROUP, GROUP)
            query = qkv[rows, cols]
            keys = spread_heads(qkv[rows, kcols], diag)
            values = spread_heads(qkv[rows, vcols], diag)
            d_row = d_att[pl.ds(p, 1), cols] / scale
            got = mm_t(two_rows(d_row), values)
            slope = got[0:1] + got[1:2]
            prob = probs[p, :, cols].astype(F32) * share
            tilted = prob * slope
            center = mm(tilted.astype(BF), ones)
            d_score = ((tilted - prob * center) * (4.0 / HEAD)).astype(BF)
            g_mixed[rows, cols] = mm(d_score, keys).astype(BF)
            g_mixed[rows, kcols] = gather_heads(mm_l(d_score, query), diag).astype(BF)
            d_rows = jnp.broadcast_to(d_row, (SPAN, GROUP)).astype(BF)
            g_mixed[rows, vcols] = gather_heads(mm_l(prob.astype(BF), d_rows), diag).astype(BF)
        return carry

    lax.fori_loop(0, OWNED, attend_back, 0)
    for j in range(3):
        got = mm(normed_t[...], g_mixed[:, pl.ds(2 * D + j * GROUP, GROUP)])
        dw_b[:, :, :, pl.ds(j * GROUP, GROUP)] = got.reshape(16, 2, WROWS, GROUP).astype(BF)
    other = w + 1 - 2 * core
    cross_b = remote(dw_b.at[:, 1 - core], core_b, csend.at[1], crecv.at[1], (other, z))
    cross_b.start()
    for j in range(6):
        cols = pl.ds(j * GROUP, GROUP)
        unit = qkv[:, cols].astype(F32)
        grad = g_mixed[:, cols].astype(F32)
        mean = mm((grad * unit).astype(BF), ones) * (1.0 / HEAD)
        back = (inv_heads[:, cols].astype(F32) * (grad - unit * mean)).astype(BF)
        g_mixed[:, cols] = back
        got = mm(normed_t[...], back)
        dw_a[:, :, :, cols] = got.reshape(16, 2, WROWS, GROUP).astype(BF)
    cross_a = remote(dw_a.at[:, 1 - core], core_a, csend.at[0], crecv.at[0], (other, z))
    cross_a.start()
    cross_b.wait_recv()

    def pair_b(i, carry):
        acc_b[i // CHIP_X, i % CHIP_X] = (
            dw_b[i, core].astype(F32) + core_b[i].astype(F32)
        ).astype(BF)
        return carry

    lax.fori_loop(0, CHIP_X * CHIP_Y, pair_b, 0)
    first = []
    for k in range(1, 4):
        ty = (y + k) % CHIP_Y
        first.append(
            remote(
                acc_b.at[ty], in_b.at[k], asend.at[1, k], arecv.at[1, k],
                ((ty * CHIP_X + x) * 2 + core, z),
            )
        )
        first[-1].start()
    for j in range(3):
        cols = pl.ds(j * GROUP, GROUP)
        d_normed[:, cols] = mm_t(g_mixed[...], wqkv[cols, :])
    cross_a.wait_recv()

    def pair_a(i, carry):
        acc_a[i % CHIP_X, i // CHIP_X] = (
            dw_a[i, core].astype(F32) + core_a[i].astype(F32)
        ).astype(BF)
        return carry

    lax.fori_loop(0, CHIP_X * CHIP_Y, pair_a, 0)
    for k in range(1, 4):
        tx = (x + k) % CHIP_X
        first.append(
            remote(
                acc_a.at[tx], in_a.at[k], asend.at[0, k], arecv.at[0, k],
                ((y * CHIP_X + tx) * 2 + core, z),
            )
        )
        first[-1].start()
    for p in range(OWNED):
        rows = pl.ds(p * SPAN, SPAN)
        length = known(p, LEN)
        unit = normed[rows, :].astype(F32)
        grad = d_normed[rows, :]
        mean = jnp.sum(grad * unit, axis=1, keepdims=True) * (1.0 / D)
        back = inv_tokens[rows, 0:1] * (grad - unit * mean)
        back = back + d_pooled[p : p + 1, :] / length.astype(F32)
        alive = iota((SPAN, D), 0) < length
        d_tokens[rows, :] = jnp.where(alive, back, 0.0).astype(BF)

    h_sent = []
    shift = iota((HIST, SPAN), 0) - iota((HIST, SPAN), 1)

    def hpiece(c, quarter, lo):
        return d_hist.at[c, quarter, pl.ds(lo, part)]

    for c in range(CHUNKS):
        for p in range(OWNED):
            put = jnp.where(shift == known(p, START), 1.0, 0.0).astype(BF)
            spread = mm(put, d_tokens[p * SPAN : (p + 1) * SPAN, c * GROUP : (c + 1) * GROUP])
            for j in range(NARROW):
                d_hist[c, j, p] = spread[j * ORROWS : (j + 1) * ORROWS].astype(BF)
        for copy in (
            remote(hpiece(c, opposite, 0), zhop.at[c, 0], hsend.at[c, 0], hrecv.at[c, 0], (w, right)),
            remote(hpiece(c, opposite, part), zhop.at[c, 1], hsend.at[c, 1], hrecv.at[c, 1], (w, left)),
            remote(hpiece(c, right, part), zfin.at[c, 1], hsend.at[c, 2], hrecv.at[c, 2], (w, right)),
            remote(hpiece(c, left, 0), zfin.at[c, 2], hsend.at[c, 3], hrecv.at[c, 3], (w, left)),
        ):
            copy.start()
            h_sent.append(copy)
    for c in range(CHUNKS):
        remote(hpiece(c, opposite, 0), zhop.at[c, 0], hsend.at[c, 0], hrecv.at[c, 0], (w, left)).wait_recv()
        for p in range(part):
            zcomb[c, 0, p] = (
                d_hist[c, right, p].astype(F32) + zhop[c, 0, p].astype(F32)
            ).astype(BF)
        on_right = remote(
            zcomb.at[c, 0], zfin.at[c, 0], hsend.at[c, 4], hrecv.at[c, 4], (w, right)
        )
        on_right.start()
        remote(hpiece(c, opposite, part), zhop.at[c, 1], hsend.at[c, 1], hrecv.at[c, 1], (w, right)).wait_recv()
        for p in range(part):
            zcomb[c, 1, p] = (
                d_hist[c, left, part + p].astype(F32) + zhop[c, 1, p].astype(F32)
            ).astype(BF)
        on_left = remote(
            zcomb.at[c, 1], zfin.at[c, 3], hsend.at[c, 5], hrecv.at[c, 5], (w, left)
        )
        on_left.start()
        h_sent.extend([on_right, on_left])
    all_back = []
    for c in range(CHUNKS):
        remote(zcomb.at[c, 0], zfin.at[c, 0], hsend.at[c, 4], hrecv.at[c, 4], (w, left)).wait_recv()
        remote(hpiece(c, right, part), zfin.at[c, 1], hsend.at[c, 2], hrecv.at[c, 2], (w, left)).wait_recv()
        remote(hpiece(c, left, 0), zfin.at[c, 2], hsend.at[c, 3], hrecv.at[c, 3], (w, right)).wait_recv()
        remote(zcomb.at[c, 1], zfin.at[c, 3], hsend.at[c, 5], hrecv.at[c, 5], (w, right)).wait_recv()
        for p in range(part):
            dsum[c, p] = (
                (d_hist[c, z, p].astype(F32) + zfin[c, 0, p].astype(F32))
                + zfin[c, 2, p].astype(F32)
            ).astype(BF)
            dsum[c, part + p] = (
                (d_hist[c, z, part + p].astype(F32) + zfin[c, 1, p].astype(F32))
                + zfin[c, 3, p].astype(F32)
            ).astype(BF)

        def send_back(k, carry):
            d = (w + k) % WIDE
            sback[c, k] = dsum[c, place_s[d]]
            remote(sback.at[c, k], rback[c].at[w], backsend.at[c], backrecv.at[c], (d, z)).start()
            return carry

        lax.fori_loop(1, WIDE, send_back, 0)
        rback[c][w] = dsum[c, place_s[w]]
        all_back.append(
            remote(
                sback.at[c, pl.ds(0, PEERS)], rback[c].at[pl.ds(0, PEERS)], backsend.at[c],
                backrecv.at[c], ((w + 1) % WIDE, z),
            )
        )

    for copy in first:
        copy.wait_recv()

    def middle(i, carry):
        mid_a[i] = (
            (acc_a[x, i].astype(F32) + in_a[1, i].astype(F32))
            + (in_a[2, i].astype(F32) + in_a[3, i].astype(F32))
        ).astype(BF)
        mid_b[i] = (
            (acc_b[y, i].astype(F32) + in_b[1, i].astype(F32))
            + (in_b[2, i].astype(F32) + in_b[3, i].astype(F32))
        ).astype(BF)
        return carry

    lax.fori_loop(0, 4, middle, 0)
    second = []
    for k in range(1, 4):
        tx = (x + k) % CHIP_X
        ty = (y + k) % CHIP_Y
        second.append(
            remote(
                mid_a.at[ty], end_a.at[k], a2send.at[0, k], a2recv.at[0, k],
                ((ty * CHIP_X + x) * 2 + core, z),
            )
        )
        second.append(
            remote(
                mid_b.at[tx], end_b.at[k], a2send.at[1, k], a2recv.at[1, k],
                ((y * CHIP_X + tx) * 2 + core, z),
            )
        )
    for copy in second:
        copy.start()
    for copy in second:
        copy.wait_recv()
    final[0:WROWS, 0:HALF] = (mid_a[y].astype(F32) + end_a[1].astype(F32)) + (
        end_a[2].astype(F32) + end_a[3].astype(F32)
    )
    final[0:WROWS, HALF:WCOLS] = (mid_b[x].astype(F32) + end_b[1].astype(F32)) + (
        end_b[2].astype(F32) + end_b[3].astype(F32)
    )
    final[WROWS : WROWS + 8, :] = jnp.zeros((8, WCOLS), F32)
    for j in range(NARROW):
        zbuf[j] = final[6 * j : 6 * j + 8, :]
    last = []
    for k in range(1, NARROW):
        t = (z + k) % NARROW
        copy = remote(zbuf.at[t], zlast.at[k], lsend.at[k], lrecv.at[k], (w, t))
        copy.start()
        last.append(copy)
    for c in range(CHUNKS):
        all_back[c].wait_recv()

        def write(a, carry):
            owner = dest[a]
            got = rback[c][jnp.maximum(owner, 0)].astype(F32)
            kept = jnp.where(jnp.full((ORROWS, GROUP), owner, I32) >= 0, got, 0.0)
            out_hist[a, :, c * GROUP : (c + 1) * GROUP] = kept.astype(BF)
            return carry

        lax.fori_loop(0, SLOTS, write, 0)
    for copy in last:
        copy.wait_recv()
    out_w[...] = (zbuf[z] + zlast[1]) + (zlast[2] + zlast[3])

    all_facts.wait_send()
    cross_a.wait_send()
    cross_b.wait_send()
    for copy in all_boxes + z_sent + e_copies + first + second + last + h_sent + all_back:
        copy.wait_send()


VM = pl.BlockSpec(memory_space=pltpu.VMEM)
SM = pl.BlockSpec(memory_space=pltpu.SMEM)
HB = pl.BlockSpec(memory_space=pl.ANY)
DMA = pltpu.SemaphoreType.DMA


def vmem(kind, *dims):
    return pltpu.VMEM(dims, kind)


def on_device(
    history, w_qkv, w_out, dest_owner, view_start, view_length, block_list, positive_offset
):
    d_history, d_w = pl.pallas_call(
        whole_kernel,
        out_shape=(
            jax.ShapeDtypeStruct((SLOTS, ORROWS, D), BF),
            jax.ShapeDtypeStruct((8, WCOLS), F32),
        ),
        in_specs=[SM, VM, VM, VM, VM, HB, HB, HB],
        out_specs=(VM, VM),
        scratch_shapes=[
            vmem(BF, D, 3 * D),
            vmem(BF, D, D),
            vmem(I32, 128, 128),
            vmem(I32, 128, 128),
            pltpu.SMEM((WIDE,), I32),
            vmem(I32, WIDE, 1, 128),
            vmem(I32, WIDE, 1, 128),
            pltpu.SMEM((WIDE, 1, 128), I32),
            pltpu.SMEM((OWNED,), I32),
            pltpu.SMEM((WIDE,), I32),
            vmem(I32, OWNED, 128),
            vmem(BF, SLOTS, QROWS, QCOLS),
            vmem(BF, CHUNKS, WIDE, CROWS, QCOLS),
            vmem(BF, WIDE, CROWS, QCOLS),
            vmem(BF, WIDE, CROWS, QCOLS),
            vmem(BF, WIDE, CROWS, QCOLS),
            vmem(BF, NARROW, OWNED, QROWS, QCOLS),
            vmem(BF, ROWS, D),
            vmem(BF, D, ROWS),
            vmem(BF, ROWS, 3 * D),
            vmem(BF, ROWS, 2 * D),
            vmem(F32, ROWS, 128),
            vmem(BF, OWNED, SPAN, D),
            vmem(F32, OWNED, D),
            vmem(F32, OWNED, D),
            vmem(F32, OWNED, D + 128),
            vmem(F32, NARROW, OWNED, D + 128),
            vmem(F32, NARROW * OWNED, D),
            vmem(F32, OWNED, D),
            vmem(F32, OWNED, D),
            vmem(BF, ROWS, 3 * D),
            vmem(F32, ROWS, D),
            vmem(BF, ROWS, D),
            vmem(BF, 16, 2, WROWS, HALF),
            vmem(BF, 16, 2, WROWS, HALF),
            vmem(BF, 16, WROWS, HALF),
            vmem(BF, 16, WROWS, HALF),
            vmem(BF, 4, 4, WROWS, HALF),
            vmem(BF, 4, 4, WROWS, HALF),
            vmem(BF, 4, 4, WROWS, HALF),
            vmem(BF, 4, 4, WROWS, HALF),
            vmem(BF, 4, WROWS, HALF),
            vmem(BF, 4, WROWS, HALF),
            vmem(BF, 4, WROWS, HALF),
            vmem(BF, 4, WROWS, HALF),
            vmem(F32, WROWS + 8, WCOLS),
            vmem(F32, NARROW, 8, WCOLS),
            vmem(F32, NARROW, 8, WCOLS),
            vmem(BF, CHUNKS, NARROW, OWNED, ORROWS, GROUP),
            vmem(BF, CHUNKS, 2, OWNED // 2, ORROWS, GROUP),
            vmem(BF, CHUNKS, 2, OWNED // 2, ORROWS, GROUP),
            vmem(BF, CHUNKS, 4, OWNED // 2, ORROWS, GROUP),
            vmem(BF, CHUNKS, OWNED, ORROWS, GROUP),
            vmem(BF, CHUNKS, WIDE, ORROWS, GROUP),
            vmem(BF, WIDE, ORROWS, GROUP),
            vmem(BF, WIDE, ORROWS, GROUP),
            vmem(BF, WIDE, ORROWS, GROUP),
            DMA((2,)), DMA, DMA, DMA((2,)),
            DMA((CHUNKS,)), DMA((CHUNKS,)),
            DMA((CHUNKS, 4)), DMA((CHUNKS, 4)),
            DMA((NARROW,)), DMA((NARROW,)),
            DMA((2,)), DMA((2,)),
            DMA((2, 4)), DMA((2, 4)),
            DMA((2, 4)), DMA((2, 4)),
            DMA((NARROW,)), DMA((NARROW,)),
            DMA((CHUNKS, 6)), DMA((CHUNKS, 6)),
            DMA((CHUNKS,)), DMA((CHUNKS,)),
        ],
        compiler_params=pltpu.CompilerParams(
            collective_id=0, has_side_effects=True, vmem_limit_bytes=VMEM_LIMIT
        ),
        name="step",
    )(
        dest_owner, view_start.T, view_length.T, positive_offset.T,
        block_list.reshape(SLOTS, 16).T, history, w_qkv, w_out,
    )
    return d_history.astype(F32), d_w[0:6, 0 : 3 * D], d_w[0:6, 3 * D : WCOLS]


def solution(mesh):
    return jax.shard_map(
        on_device,
        mesh=mesh,
        in_specs=(
            P("wide", None, None),
            P(),
            P(),
            P("wide"),
            P("wide", "narrow"),
            P("wide", "narrow"),
            P("wide", "narrow", None, None),
            P("wide", "narrow"),
        ),
        out_specs=(
            P("wide", "narrow", None),
            P(("wide", "narrow"), None),
            P(("wide", "narrow"), None),
        ),
        check_vma=False,
    )
```

```python
import jax
import jax.numpy as jnp
from jax import lax
from jax.experimental import pallas as pl
from jax.experimental.pallas import tpu as pltpu
from jax.sharding import PartitionSpec as P

BF = jnp.bfloat16
F32 = jnp.float32
I32 = jnp.int32
MESH = pl.DeviceIdType.MESH

WIDE = 32
NARROW = 4
CHIP_X = 4
CHIP_Y = 4
OWNED = 8
SLOTS = 16
D = 768
HEAD = 64
SPAN = 64
HIST = 96
GROUP = 256
ROWS = OWNED * SPAN
QROWS = HIST // 2
QCOLS = D // 2
ORROWS = HIST // NARROW
WROWS = D // WIDE
WCOLS = 4 * D

LIVE, LEN, OFF, START, BLOCKS = 0, 1, 2, 3, 8
BOXES = ((0, 16, 0, 384), (16, 16, 0, 384), (32, 16, 0, 256), (32, 16, 256, 128))
NBOX = len(BOXES)
BACKS = ((0, 128), (128, 256), (384, 256), (640, 128))
NBACK = len(BACKS)
PAIR = 2
PEERS = WIDE - 1
EPS = 1e-06
VMEM_LIMIT = 60 * 1024 * 1024


def mm(a, b):
    return jnp.dot(a, b, preferred_element_type=F32)


def mm_t(a, b):
    return lax.dot_general(a, b, (((1,), (1,)), ((), ())), preferred_element_type=F32)


def mm_l(a, b):
    return lax.dot_general(a, b, (((0,), (0,)), ((), ())), preferred_element_type=F32)


def split_hi_lo(x):
    hi = x.astype(BF)
    return hi, (x - hi.astype(F32)).astype(BF)


def iota(shape, dim):
    return lax.broadcasted_iota(I32, shape, dim)


def head_diag():
    shape = (GROUP, GROUP)
    return (iota(shape, 0) // HEAD) == (iota(shape, 1) // HEAD)


def spread_heads(x, diag):
    return jnp.where(diag, jnp.concatenate([x, x, x, x], axis=0), jnp.zeros((), x.dtype))


def gather_heads(full, diag):
    kept = jnp.where(diag, full, 0.0)
    return (kept[0:64] + kept[64:128]) + (kept[128:192] + kept[192:256])


def whole_kernel(
    dest, starts, lengths, offsets, lists, hist, wqkv_hbm, wout_hbm,
    out_hist, out_w,
    wqkv, wout, fact_t, fact, slot_s, message, frecv, fsm, pick_s, place_s, facts8,
    hbuf, crop,
    normed, normed_t, qkv, inv_heads, inv_tokens, probs, col_w, pooled, mean_att,
    mine, everyone, d_embed, d_pooled, d_att, g_mixed, d_normed, d_tokens,
    dw, core_in, acc, ring, mid, ends, final, zbuf, zlast,
    sbuf_0, sbuf_1, sbuf_2, sbuf_3, rbuf_0, rbuf_1, rbuf_2, rbuf_3,
    hist_0, hist_1, hist_2, hist_3, zin_0, zin_1, zin_2, zin_3,
    dsum_0, dsum_1, dsum_2, dsum_3, sback_0, sback_1, sback_2, sback_3,
    rback_0, rback_1, rback_2, rback_3,
    wsem, lsem, fsem, factsem, boxsend, boxrecv, zsend, zrecv, esend, erecv,
    csend, crecv, asend, arecv, a2send, a2recv, lsend, lrecv,
    hsend, hrecv, backsend, backrecv,
):
    w = lax.axis_index("wide")
    z = lax.axis_index("narrow")
    core = w % 2
    x = (w // 2) % CHIP_X
    y = w // (2 * CHIP_X)
    def remote(src, dst, send, recv, to):
        return pltpu.make_async_remote_copy(
            src_ref=src, dst_ref=dst, send_sem=send, recv_sem=recv, device_id=to,
            device_id_type=MESH,
        )

    sbuf = (sbuf_0, sbuf_1, sbuf_2, sbuf_3)
    rbuf = (rbuf_0, rbuf_1, rbuf_2, rbuf_3)
    d_hist = (hist_0, hist_1, hist_2, hist_3)
    zin = (zin_0, zin_1, zin_2, zin_3)
    dsum = (dsum_0, dsum_1, dsum_2, dsum_3)
    sback = (sback_0, sback_1, sback_2, sback_3)
    rback = (rback_0, rback_1, rback_2, rback_3)

    load = pltpu.make_async_copy(
        hist.at[:, pl.ds(QROWS * (z // 2), QROWS), pl.ds(QCOLS * (z % 2), QCOLS)], hbuf, lsem
    )
    load.start()
    barrier = pltpu.get_barrier_semaphore()

    def greet(k, c):
        pl.semaphore_signal(barrier, inc=1, device_id=((w + k) % WIDE, z), device_id_type=MESH)
        return c

    lax.fori_loop(1, WIDE, greet, 0)
    for k in range(1, NARROW):
        pl.semaphore_signal(barrier, inc=1, device_id=(w, (z + k) % NARROW), device_id_type=MESH)
    load_qkv = pltpu.make_async_copy(wqkv_hbm, wqkv, wsem.at[0])
    load_out = pltpu.make_async_copy(wout_hbm, wout, wsem.at[1])
    load_qkv.start()
    load_out.start()

    fact_t[...] = jnp.zeros((128, 128), I32)
    fact_t[LIVE : LIVE + 1, :] = jnp.ones((1, 128), I32)
    fact_t[LEN : LEN + 1, 0:SLOTS] = lengths[...]
    fact_t[OFF : OFF + 1, 0:SLOTS] = offsets[...]
    fact_t[START : START + 1, 0:SLOTS] = starts[...]
    fact_t[BLOCKS : BLOCKS + 16, 0:SLOTS] = lists[...]
    fact[...] = fact_t[...].T
    owners = [dest[a] for a in range(SLOTS)]

    def find(d, c):
        slot = jnp.int32(0)
        live = jnp.int32(0)
        for a in range(SLOTS):
            hit = owners[a] == d
            slot = jnp.where(hit, a, slot)
            live = jnp.where(hit, 1, live)
        slot_s[d] = slot
        message[d] = fact[pl.ds(slot, 1), :] * live
        return c

    lax.fori_loop(0, WIDE, find, 0)
    load.wait()

    def fill(k, carry):
        slot = slot_s[(w + k) % WIDE]
        for c, (r0, nr, c0, nc) in enumerate(BOXES):
            sbuf[c][k] = hbuf[slot, r0 : r0 + nr, c0 : c0 + nc]
        return carry

    lax.fori_loop(1, WIDE, fill, 0)
    frecv[w] = message[w]
    for c, (r0, nr, c0, nc) in enumerate(BOXES):
        rbuf[c][w] = hbuf[slot_s[w], r0 : r0 + nr, c0 : c0 + nc]
    pl.semaphore_wait(barrier, PEERS + NARROW - 1)

    def send_facts(k, c):
        d = (w + k) % WIDE
        remote(message.at[d], frecv.at[w], factsem.at[0], factsem.at[1], (d, z)).start()
        return c

    lax.fori_loop(1, WIDE, send_facts, 0)
    for c in range(NBOX):

        def send_box(k, carry):
            d = (w + k) % WIDE
            remote(sbuf[c].at[k], rbuf[c].at[w], boxsend.at[c], boxrecv.at[c], (d, z)).start()
            return carry

        lax.fori_loop(1, WIDE, send_box, 0)
    all_facts = remote(
        message.at[pl.ds(0, PEERS)], frecv.at[pl.ds(0, PEERS)], factsem.at[0], factsem.at[1],
        ((w + 1) % WIDE, z),
    )
    all_facts.wait_recv()
    down = pltpu.make_async_copy(frecv, fsm, fsem)
    down.start()
    down.wait()

    def scan(s, carry):
        count, picks = carry
        live = fsm[s, 0, LIVE]
        place_s[s] = jnp.minimum(count, OWNED - 1)
        picks = tuple(jnp.where((live > 0) & (count == p), s, picks[p]) for p in range(OWNED))
        return count + live, picks

    _, picks = lax.fori_loop(
        0, WIDE, scan, (jnp.int32(0), tuple(jnp.int32(0) for _ in range(OWNED)))
    )
    for p in range(OWNED):
        pick_s[p] = picks[p]
        facts8[p : p + 1, :] = frecv[picks[p]]

    def known(p, which):
        return fsm[pick_s[p], 0, which]

    def spread_z(c, quarter, k, to):
        r0, nr, c0, nc = BOXES[c]
        where = crop.at[quarter, :, pl.ds(r0, nr), pl.ds(c0, nc)]
        return remote(where, where, zsend.at[c, k], zrecv.at[c, k], (w, to))

    all_boxes = []
    z_sent = []
    for c, (r0, nr, c0, nc) in enumerate(BOXES):
        boxes = remote(
            sbuf[c].at[pl.ds(0, PEERS)], rbuf[c].at[pl.ds(0, PEERS)], boxsend.at[c],
            boxrecv.at[c], ((w + 1) % WIDE, z),
        )
        all_boxes.append(boxes)
        boxes.wait_recv()
        for p in range(OWNED):
            crop[z, p, r0 : r0 + nr, c0 : c0 + nc] = rbuf[c][picks[p]]
        for k in (2, 1, 3):
            z_sent.append(spread_z(c, z, k, (z + k) % NARROW))
            z_sent[-1].start()
    for c in range(NBOX):
        for k in range(1, NARROW):
            s = (z + NARROW - k) % NARROW
            spread_z(c, s, k, s).wait_recv()

    diag = head_diag()
    ones = jnp.where(diag, 1.0, 0.0).astype(BF)
    row48 = iota((SPAN, QROWS), 0)
    col48 = iota((SPAN, QROWS), 1)
    for p in range(OWNED):
        start = known(p, START)
        length = known(p, LEN)
        rows = pl.ds(p * SPAN, SPAN)
        source = row48 + start
        alive = row48 < length
        top = jnp.where((col48 == source) & alive, 1.0, 0.0).astype(BF)
        low = jnp.where((col48 + QROWS == source) & alive, 1.0, 0.0).astype(BF)
        lhs = mm(top, crop[0, p]) + mm(low, crop[2, p])
        rhs = mm(top, crop[1, p]) + mm(low, crop[3, p])
        square = jnp.sum(lhs * lhs, axis=1, keepdims=True) + jnp.sum(
            rhs * rhs, axis=1, keepdims=True
        )
        inv = lax.rsqrt(square * (1.0 / D) + EPS)
        normed[rows, 0:QCOLS] = (lhs * inv).astype(BF)
        normed[rows, QCOLS:D] = (rhs * inv).astype(BF)
        inv_tokens[rows, :] = jnp.broadcast_to(inv, (SPAN, 128))
        scale = length.astype(F32)
        pooled[p : p + 1, 0:QCOLS] = jnp.sum(lhs, axis=0, keepdims=True) / scale
        pooled[p : p + 1, QCOLS:D] = jnp.sum(rhs, axis=0, keepdims=True) / scale
    load_qkv.wait()
    load_out.wait()
    for j in range(9):
        cols = pl.ds(j * GROUP, GROUP)
        mixed = mm(normed[...], wqkv[:, cols])
        if j < 6:
            square = mm((mixed * mixed).astype(BF), ones)
            inv = lax.rsqrt(square * (1.0 / HEAD) + EPS)
            qkv[:, cols] = (mixed * inv).astype(BF)
            inv_heads[:, cols] = inv.astype(BF)
        else:
            qkv[:, cols] = mixed.astype(BF)

    ones_lane = iota((1, GROUP), 1) % SPAN
    query_block = ones_lane // 16
    key_row = iota((SPAN, GROUP), 0)
    key_block = key_row // 16
    causal = key_row <= ones_lane

    def attend(p):
        rows = pl.ds(pl.multiple_of(p * SPAN, SPAN), SPAN)
        length = known(p, LEN)
        listed = None
        for j in range(4):
            want = [known(p, BLOCKS + 4 * b + j) for b in range(4)]
            want = jnp.where(
                query_block < 2,
                jnp.where(query_block == 0, want[0], want[1]),
                jnp.where(query_block == 2, want[2], want[3]),
            )
            hit = key_block == want
            listed = hit if listed is None else listed | hit
        allowed = jnp.where(listed & causal, 1.0, 0.0)
        alive = jnp.where(ones_lane < length, 1.0, 0.0)
        scale = length.astype(F32)
        for g in range(3):
            cols = pl.ds(g * GROUP, GROUP)
            query = spread_heads(qkv[rows, cols], diag)
            keys = qkv[rows, pl.ds(D + g * GROUP, GROUP)]
            weight = jnp.exp(mm_t(keys, query) * (4.0 / HEAD)) * allowed
            total = jnp.sum(weight, axis=0, keepdims=True)
            prob = (weight * (alive / total)).astype(BF)
            probs[p, :, cols] = prob
            column = mm(prob, ones) / scale
            col_w[rows, cols] = column
            values = qkv[rows, pl.ds(2 * D + g * GROUP, GROUP)].astype(F32)
            mean_att[pl.ds(p, 1), cols] = jnp.sum(column * values, axis=0, keepdims=True)

    def attend_some(i, carry):
        for q in range(PAIR):
            attend(i * PAIR + q)
        return carry

    lax.fori_loop(0, OWNED // PAIR, attend_some, 0)
    att_hi, att_lo = split_hi_lo(mean_att[...])
    pooled[...] += mm(att_hi, wout[...]) + mm(att_lo, wout[...])

    pool = pooled[...]
    inv_pool = lax.rsqrt(jnp.sum(pool * pool, axis=1, keepdims=True) + EPS)
    embed = pool * inv_pool
    mine[:, 0:D] = embed
    mine[:, D : D + 128] = jnp.broadcast_to(facts8[:, OFF : OFF + 1].astype(F32), (OWNED, 128))
    e_copies = []
    for k in range(1, NARROW):
        copy = remote(
            mine, everyone.at[z], esend.at[k], erecv.at[k], (w, (z + k) % NARROW)
        )
        copy.start()
        e_copies.append(copy)
    everyone[z] = mine[...]
    normed_t[...] = normed[...].T
    for k in range(1, NARROW):
        s = (z + NARROW - k) % NARROW
        remote(mine, everyone.at[s], esend.at[k], erecv.at[k], (w, s)).wait_recv()
    total = NARROW * OWNED
    full = everyone[...].reshape(total, D + 128)
    group = full[:, 0:D]
    offset = full[:, D : D + total].astype(I32)
    high = lax.Precision.HIGHEST
    logit = (
        lax.dot_general(
            group, group, (((1,), (1,)), ((), ())), precision=high, preferred_element_type=F32
        )
        / 0.1
    )
    row = iota((total, total), 0)
    col = iota((total, total), 1)
    positive = ((row // OWNED + offset) % NARROW) * OWNED + row % OWNED
    weight = jnp.where(row != col, jnp.exp(logit), 0.0)
    prob = weight / jnp.sum(weight, axis=1, keepdims=True)
    coef = (512.0 / 0.1) * (prob - jnp.where(col == positive, 1.0, 0.0))
    d_embed[...] = jnp.dot(
        coef, group, precision=high, preferred_element_type=F32
    ) + lax.dot_general(
        coef, group, (((0,), (0,)), ((), ())), precision=high, preferred_element_type=F32
    )
    own = d_embed[pl.ds(pl.multiple_of(OWNED * z, OWNED), OWNED), :]
    d_pooled[...] = inv_pool * (own - embed * jnp.sum(own * embed, axis=1, keepdims=True))

    hi, lo = split_hi_lo(d_pooled[...])
    d_att[...] = mm_t(hi, wout[...]) + mm_t(lo, wout[...])
    other = w + 1 - 2 * core
    w_sent = []

    def put_dw(t, j, got):
        dw[t, :, :, :, pl.ds(j * GROUP, GROUP)] = got.reshape(16, 2, WROWS, GROUP).astype(BF)

    def cross(t):
        return remote(dw.at[t, :, 1 - core], core_in.at[t], csend.at[t], crecv.at[t], (other, z))

    def along(t, first, k):
        if (t in (0, 3)) == first:
            return ((y * CHIP_X + (x + k) % CHIP_X) * 2 + core, z), (x + k) % CHIP_X
        return ((((y + k) % CHIP_Y) * CHIP_X + x) * 2 + core, z), (y + k) % CHIP_Y

    def start_cross(t):
        w_sent.append(cross(t))
        w_sent[-1].start()

    def start_first(t):
        cross(t).wait_recv()

        def pair(i, carry):
            at = (i % CHIP_X, i // CHIP_X) if t in (0, 3) else (i // CHIP_X, i % CHIP_X)
            acc[t, at[0], at[1]] = (
                dw[t, i, core].astype(F32) + core_in[t, i].astype(F32)
            ).astype(BF)
            return carry

        lax.fori_loop(0, CHIP_X * CHIP_Y, pair, 0)
        for k in (2, 1, 3):
            to, at = along(t, True, k)
            w_sent.append(
                remote(acc.at[t, at], ring.at[t, k], asend.at[t, k], arecv.at[t, k], to)
            )
            w_sent[-1].start()

    def start_second(t):
        for k in range(1, 4):
            to, at = along(t, True, k)
            remote(acc.at[t, at], ring.at[t, k], asend.at[t, k], arecv.at[t, k], to).wait_recv()
        here = along(t, True, 0)[1]

        def middle(i, carry):
            mid[t, i] = (
                (acc[t, here, i].astype(F32) + ring[t, 1, i].astype(F32))
                + (ring[t, 2, i].astype(F32) + ring[t, 3, i].astype(F32))
            ).astype(BF)
            return carry

        lax.fori_loop(0, 4, middle, 0)
        for k in (2, 1, 3):
            to, at = along(t, False, k)
            w_sent.append(
                remote(mid.at[t, at], ends.at[t, k], a2send.at[t, k], a2recv.at[t, k], to)
            )
            w_sent[-1].start()

    def finish_second(t):
        for k in range(1, 4):
            to, at = along(t, False, k)
            remote(mid.at[t, at], ends.at[t, k], a2send.at[t, k], a2recv.at[t, k], to).wait_recv()
        here = along(t, False, 0)[1]
        final[0:WROWS, t * D : (t + 1) * D] = (
            mid[t, here].astype(F32) + ends[t, 1].astype(F32)
        ) + (ends[t, 2].astype(F32) + ends[t, 3].astype(F32))

    both = jnp.concatenate([att_hi, att_lo], axis=0)
    twice = jnp.concatenate([hi, hi], axis=0)
    for j in range(3):
        put_dw(3, j, mm_l(both, twice[:, j * GROUP : (j + 1) * GROUP]))
    start_cross(3)
    for p in range(OWNED):
        rows = pl.ds(p * SPAN, SPAN)
        g_mixed[rows, 2 * D : 3 * D] = (col_w[rows, :] * d_att[p : p + 1, :]).astype(BF)
    for j in range(3):
        put_dw(2, j, mm(normed_t[...], g_mixed[:, pl.ds(2 * D + j * GROUP, GROUP)]))
    start_cross(2)
    start_first(3)

    def attend_back(p):
        rows = pl.ds(pl.multiple_of(p * SPAN, SPAN), SPAN)
        scale = known(p, LEN).astype(F32)
        for g in range(3):
            cols = pl.ds(g * GROUP, GROUP)
            kcols = pl.ds(D + g * GROUP, GROUP)
            query = spread_heads(qkv[rows, cols], diag)
            keys = qkv[rows, kcols]
            values = qkv[rows, pl.ds(2 * D + g * GROUP, GROUP)].astype(F32)
            d_row = d_att[pl.ds(p, 1), cols] / scale
            slope = mm((values * d_row).astype(BF), ones)
            prob = probs[p, :, cols].astype(F32)
            tilted = prob * slope
            center = jnp.sum(tilted, axis=0, keepdims=True)
            d_score = ((tilted - prob * center) * (4.0 / HEAD)).astype(BF)
            g_mixed[rows, kcols] = mm(d_score, query).astype(BF)
            g_mixed[rows, cols] = gather_heads(mm_l(d_score, keys), diag).astype(BF)

    def attend_back_some(i, carry):
        for q in range(PAIR):
            attend_back(i * PAIR + q)
        return carry

    lax.fori_loop(0, OWNED // PAIR // 2, attend_back_some, 0)
    start_first(2)
    lax.fori_loop(OWNED // PAIR // 2, OWNED // PAIR, attend_back_some, 0)
    for j in range(6):
        cols = pl.ds(j * GROUP, GROUP)
        unit = qkv[:, cols].astype(F32)
        grad = g_mixed[:, cols].astype(F32)
        mean = mm((grad * unit).astype(BF), ones) * (1.0 / HEAD)
        g_mixed[:, cols] = (inv_heads[:, cols].astype(F32) * (grad - unit * mean)).astype(BF)
    for j in range(3):
        cols = pl.ds(j * GROUP, GROUP)
        d_normed[:, cols] = mm_t(g_mixed[...], wqkv[cols, :])
    for p in range(OWNED):
        rows = pl.ds(p * SPAN, SPAN)
        length = known(p, LEN)
        unit = normed[rows, :].astype(F32)
        grad = d_normed[rows, :]
        mean = jnp.sum(grad * unit, axis=1, keepdims=True) * (1.0 / D)
        back = inv_tokens[rows, 0:1] * (grad - unit * mean)
        back = back + d_pooled[p : p + 1, :] / length.astype(F32)
        alive = iota((SPAN, D), 0) < length
        d_tokens[rows, :] = jnp.where(alive, back, 0.0).astype(BF)

    h_sent = []
    shift = iota((HIST, SPAN), 0) - iota((HIST, SPAN), 1)
    puts = [jnp.where(shift == known(p, START), 1.0, 0.0).astype(BF) for p in range(OWNED)]
    for c, (c0, nc) in enumerate(BACKS):
        for p in range(OWNED):
            spread = mm(puts[p], d_tokens[p * SPAN : (p + 1) * SPAN, c0 : c0 + nc])
            for j in range(NARROW):
                d_hist[c][j, p] = spread[j * ORROWS : (j + 1) * ORROWS].astype(BF)
        for k in (2, 1, 3):
            t = (z + k) % NARROW
            h_sent.append(remote(d_hist[c].at[t], zin[c].at[k], hsend.at[c, k], hrecv.at[c, k], (w, t)))
            h_sent[-1].start()
    for t in (0, 1):
        for j in range(3):
            put_dw(t, j, mm(normed_t[...], g_mixed[:, pl.ds(t * D + j * GROUP, GROUP)]))
        start_cross(t)
    start_second(3)
    start_second(2)
    start_first(0)
    start_first(1)
    all_back = []
    for c, (c0, nc) in enumerate(BACKS):
        for k in range(1, NARROW):
            s = (z + NARROW - k) % NARROW
            remote(d_hist[c].at[s], zin[c].at[k], hsend.at[c, k], hrecv.at[c, k], (w, s)).wait_recv()
        for p in range(OWNED):
            dsum[c][p] = (
                (d_hist[c][z, p].astype(F32) + zin[c][1, p].astype(F32))
                + (zin[c][2, p].astype(F32) + zin[c][3, p].astype(F32))
            ).astype(BF)

        def send_back(k, carry):
            d = (w + k) % WIDE
            sback[c][k] = dsum[c][place_s[d]]
            remote(sback[c].at[k], rback[c].at[w], backsend.at[c], backrecv.at[c], (d, z)).start()
            return carry

        lax.fori_loop(1, WIDE, send_back, 0)
        rback[c][w] = dsum[c][place_s[w]]
        all_back.append(
            remote(
                sback[c].at[pl.ds(0, PEERS)], rback[c].at[pl.ds(0, PEERS)], backsend.at[c],
                backrecv.at[c], ((w + 1) % WIDE, z),
            )
        )
        if c == 1:
            start_second(0)
            start_second(1)
    final[WROWS : WROWS + 8, :] = jnp.zeros((8, WCOLS), F32)
    for t in (3, 2, 0, 1):
        finish_second(t)
    for j in range(NARROW):
        zbuf[j] = final[6 * j : 6 * j + 8, :]
    last = []
    for k in range(1, NARROW):
        t = (z + k) % NARROW
        copy = remote(zbuf.at[t], zlast.at[k], lsend.at[k], lrecv.at[k], (w, t))
        copy.start()
        last.append(copy)
    for c, (c0, nc) in enumerate(BACKS):
        all_back[c].wait_recv()

        def write(a, carry):
            owner = dest[a]
            got = rback[c][jnp.maximum(owner, 0)].astype(F32)
            kept = jnp.where(jnp.full((ORROWS, nc), owner, I32) >= 0, got, 0.0)
            out_hist[a, :, c0 : c0 + nc] = kept.astype(BF)
            return carry

        lax.fori_loop(0, SLOTS, write, 0)
    for copy in last:
        copy.wait_recv()
    out_w[...] = (zbuf[z] + zlast[1]) + (zlast[2] + zlast[3])

    all_facts.wait_send()
    for copy in all_boxes + z_sent + e_copies + w_sent + last + h_sent + all_back:
        copy.wait_send()


def finish_kernel(hist, d_w, out_hist, out_qkv, out_out):
    out_hist[...] = hist[...].astype(F32)
    out_qkv[...] = d_w[0:6, 0 : 3 * D]
    out_out[...] = d_w[0:6, 3 * D : WCOLS]


VM = pl.BlockSpec(memory_space=pltpu.VMEM)
SM = pl.BlockSpec(memory_space=pltpu.SMEM)
HB = pl.BlockSpec(memory_space=pl.ANY)
DMA = pltpu.SemaphoreType.DMA


def vmem(kind, *dims):
    return pltpu.VMEM(dims, kind)


def on_device(
    history, w_qkv, w_out, dest_owner, view_start, view_length, block_list, positive_offset
):
    d_history, d_w = pl.pallas_call(
        whole_kernel,
        out_shape=(
            jax.ShapeDtypeStruct((SLOTS, ORROWS, D), BF),
            jax.ShapeDtypeStruct((8, WCOLS), F32),
        ),
        in_specs=[SM, VM, VM, VM, VM, HB, HB, HB],
        out_specs=(VM, VM),
        scratch_shapes=[
            vmem(BF, D, 3 * D),
            vmem(BF, D, D),
            vmem(I32, 128, 128),
            vmem(I32, 128, 128),
            pltpu.SMEM((WIDE,), I32),
            vmem(I32, WIDE, 1, 128),
            vmem(I32, WIDE, 1, 128),
            pltpu.SMEM((WIDE, 1, 128), I32),
            pltpu.SMEM((OWNED,), I32),
            pltpu.SMEM((WIDE,), I32),
            vmem(I32, OWNED, 128),
            vmem(BF, SLOTS, QROWS, QCOLS),
            vmem(BF, NARROW, OWNED, QROWS, QCOLS),
            vmem(BF, ROWS, D),
            vmem(BF, D, ROWS),
            vmem(BF, ROWS, 3 * D),
            vmem(BF, ROWS, 2 * D),
            vmem(F32, ROWS, 128),
            vmem(BF, OWNED, SPAN, D),
            vmem(F32, ROWS, D),
            vmem(F32, OWNED, D),
            vmem(F32, OWNED, D),
            vmem(F32, OWNED, D + 128),
            vmem(F32, NARROW, OWNED, D + 128),
            vmem(F32, NARROW * OWNED, D),
            vmem(F32, OWNED, D),
            vmem(F32, OWNED, D),
            vmem(BF, ROWS, 3 * D),
            vmem(F32, ROWS, D),
            vmem(BF, ROWS, D),
            vmem(BF, 4, 16, 2, WROWS, D),
            vmem(BF, 4, 16, WROWS, D),
            vmem(BF, 4, 4, 4, WROWS, D),
            vmem(BF, 4, 4, 4, WROWS, D),
            vmem(BF, 4, 4, WROWS, D),
            vmem(BF, 4, 4, WROWS, D),
            vmem(F32, WROWS + 8, WCOLS),
            vmem(F32, NARROW, 8, WCOLS),
            vmem(F32, NARROW, 8, WCOLS),
            *[vmem(BF, WIDE, nr, nc) for _, nr, _, nc in BOXES],
            *[vmem(BF, WIDE, nr, nc) for _, nr, _, nc in BOXES],
            *[vmem(BF, NARROW, OWNED, ORROWS, nc) for _, nc in BACKS],
            *[vmem(BF, NARROW, OWNED, ORROWS, nc) for _, nc in BACKS],
            *[vmem(BF, OWNED, ORROWS, nc) for _, nc in BACKS],
            *[vmem(BF, WIDE, ORROWS, nc) for _, nc in BACKS],
            *[vmem(BF, WIDE, ORROWS, nc) for _, nc in BACKS],
            DMA((2,)), DMA, DMA, DMA((2,)),
            DMA((NBOX,)), DMA((NBOX,)),
            DMA((NBOX, 4)), DMA((NBOX, 4)),
            DMA((NARROW,)), DMA((NARROW,)),
            DMA((4,)), DMA((4,)),
            DMA((4, 4)), DMA((4, 4)),
            DMA((4, 4)), DMA((4, 4)),
            DMA((NARROW,)), DMA((NARROW,)),
            DMA((NBACK, 4)), DMA((NBACK, 4)),
            DMA((NBACK,)), DMA((NBACK,)),
        ],
        compiler_params=pltpu.CompilerParams(
            collective_id=0, has_side_effects=True, vmem_limit_bytes=VMEM_LIMIT
        ),
        name="step",
    )(
        dest_owner, view_start.T, view_length.T, positive_offset.T,
        block_list.reshape(SLOTS, 16).T, history, w_qkv, w_out,
    )
    return pl.pallas_call(
        finish_kernel,
        out_shape=(
            jax.ShapeDtypeStruct((SLOTS, ORROWS, D), F32),
            jax.ShapeDtypeStruct((6, 3 * D), F32),
            jax.ShapeDtypeStruct((6, D), F32),
        ),
        in_specs=[VM, VM],
        out_specs=(VM, VM, VM),
        name="finish",
    )(d_history, d_w)


def solution(mesh):
    return jax.shard_map(
        on_device,
        mesh=mesh,
        in_specs=(
            P("wide", None, None),
            P(),
            P(),
            P("wide"),
            P("wide", "narrow"),
            P("wide", "narrow"),
            P("wide", "narrow", None, None),
            P("wide", "narrow"),
        ),
        out_specs=(
            P("wide", "narrow", None),
            P(("wide", "narrow"), None),
            P(("wide", "narrow"), None),
        ),
        check_vma=False,
    )
```

```python
import jax
import jax.numpy as jnp
from jax import lax
from jax.experimental import pallas as pl
from jax.experimental.pallas import tpu as pltpu
from jax.sharding import PartitionSpec as P

BF = jnp.bfloat16
F32 = jnp.float32
I32 = jnp.int32
MESH = pl.DeviceIdType.MESH

WIDE = 32
NARROW = 4
CHIP_X = 4
CHIP_Y = 4
OWNED = 8
SLOTS = 16
D = 768
HEAD = 64
SPAN = 64
HIST = 96
GROUP = 256
ROWS = OWNED * SPAN
QROWS = HIST // 2
QCOLS = D // 2
ORROWS = HIST // NARROW
WROWS = D // WIDE
WCOLS = 4 * D

LIVE, LEN, OFF, START, BLOCKS = 0, 1, 2, 3, 8
BOXES = (
    (0, 16, 0, 128, False),
    (0, 16, 128, 256, False),
    (16, 16, 0, 384, True),
    (32, 16, 0, 256, True),
    (32, 16, 256, 128, False),
)
NBOX = len(BOXES)
BACKS = ((0, 128, False), (128, 256, False), (384, 256, False), (640, 128, False))
NBACK = len(BACKS)
PAIR = 4
PEERS = WIDE - 1
EPS = 1e-06
VMEM_LIMIT = 60 * 1024 * 1024


def mm(a, b):
    return jnp.dot(a, b, preferred_element_type=F32)


def mm_t(a, b):
    return lax.dot_general(a, b, (((1,), (1,)), ((), ())), preferred_element_type=F32)


def mm_l(a, b):
    return lax.dot_general(a, b, (((0,), (0,)), ((), ())), preferred_element_type=F32)


def split_hi_lo(x):
    hi = x.astype(BF)
    return hi, (x - hi.astype(F32)).astype(BF)


def iota(shape, dim):
    return lax.broadcasted_iota(I32, shape, dim)


def head_diag():
    shape = (GROUP, GROUP)
    return (iota(shape, 0) // HEAD) == (iota(shape, 1) // HEAD)


def spread_heads(x, diag):
    return jnp.where(diag, jnp.concatenate([x, x, x, x], axis=0), jnp.zeros((), x.dtype))


def gather_heads(full, diag):
    kept = jnp.where(diag, full, 0.0)
    return (kept[0:64] + kept[64:128]) + (kept[128:192] + kept[192:256])


def whole_kernel(
    dest, starts, lengths, offsets, lists, hist, wqkv_hbm, wout_hbm,
    out_hist, out_w,
    wqkv, wout, fact_t, fact, slot_s, message, frecv, fsm, pick_s, place_s, facts8,
    hbuf, crop,
    normed, normed_t, qkv, inv_heads, inv_tokens, probs, col_w, pooled, mean_att,
    mine, everyone, d_embed, d_pooled, d_att, g_mixed, d_normed, d_tokens,
    dw, core_in, acc, ring, mid, ends, final, zbuf, zlast,
    sbuf_0, sbuf_1, sbuf_2, sbuf_3, sbuf_4, rbuf_0, rbuf_1, rbuf_2, rbuf_3, rbuf_4,
    hist_0, hist_1, hist_2, hist_3, zin_0, zin_1, zin_2, zin_3, comb_0, comb_1, comb_2, comb_3,
    dsum_0, dsum_1, dsum_2, dsum_3, sback_0, sback_1, sback_2, sback_3,
    rback_0, rback_1, rback_2, rback_3,
    wsem, lsem, fsem, factsem, boxsend, boxrecv, zsend, zrecv, esend, erecv,
    csend, crecv, asend, arecv, a2send, a2recv, lsend, lrecv,
    hsend, hrecv, backsend, backrecv,
):
    w = lax.axis_index("wide")
    z = lax.axis_index("narrow")
    core = w % 2
    x = (w // 2) % CHIP_X
    y = w // (2 * CHIP_X)
    def remote(src, dst, send, recv, to):
        return pltpu.make_async_remote_copy(
            src_ref=src, dst_ref=dst, send_sem=send, recv_sem=recv, device_id=to,
            device_id_type=MESH,
        )

    sbuf = (sbuf_0, sbuf_1, sbuf_2, sbuf_3, sbuf_4)
    rbuf = (rbuf_0, rbuf_1, rbuf_2, rbuf_3, rbuf_4)
    d_hist = (hist_0, hist_1, hist_2, hist_3)
    zin = (zin_0, zin_1, zin_2, zin_3)
    comb = (comb_0, comb_1, comb_2, comb_3)
    right = (z + 1) % NARROW
    left = (z + 3) % NARROW
    opposite = (z + 2) % NARROW
    part = OWNED // 2
    dsum = (dsum_0, dsum_1, dsum_2, dsum_3)
    sback = (sback_0, sback_1, sback_2, sback_3)
    rback = (rback_0, rback_1, rback_2, rback_3)

    load = pltpu.make_async_copy(
        hist.at[:, pl.ds(QROWS * (z // 2), QROWS), pl.ds(QCOLS * (z % 2), QCOLS)], hbuf, lsem
    )
    load.start()
    barrier = pltpu.get_barrier_semaphore()

    def greet(k, c):
        pl.semaphore_signal(barrier, inc=1, device_id=((w + k) % WIDE, z), device_id_type=MESH)
        return c

    lax.fori_loop(1, WIDE, greet, 0)
    for k in range(1, NARROW):
        pl.semaphore_signal(barrier, inc=1, device_id=(w, (z + k) % NARROW), device_id_type=MESH)
    load_qkv = pltpu.make_async_copy(wqkv_hbm, wqkv, wsem.at[0])
    load_out = pltpu.make_async_copy(wout_hbm, wout, wsem.at[1])
    load_qkv.start()
    load_out.start()

    fact_t[...] = jnp.zeros((128, 128), I32)
    fact_t[LIVE : LIVE + 1, :] = jnp.ones((1, 128), I32)
    fact_t[LEN : LEN + 1, 0:SLOTS] = lengths[...]
    fact_t[OFF : OFF + 1, 0:SLOTS] = offsets[...]
    fact_t[START : START + 1, 0:SLOTS] = starts[...]
    fact_t[BLOCKS : BLOCKS + 16, 0:SLOTS] = lists[...]
    fact[...] = fact_t[...].T
    owners = [dest[a] for a in range(SLOTS)]

    def find(d, c):
        slot = jnp.int32(0)
        live = jnp.int32(0)
        for a in range(SLOTS):
            hit = owners[a] == d
            slot = jnp.where(hit, a, slot)
            live = jnp.where(hit, 1, live)
        slot_s[d] = slot
        message[d] = fact[pl.ds(slot, 1), :] * live
        return c

    lax.fori_loop(0, WIDE, find, 0)
    load.wait()

    def fill(k, carry):
        slot = slot_s[(w + k) % WIDE]
        for c, (r0, nr, c0, nc, ring_z) in enumerate(BOXES):
            sbuf[c][k] = hbuf[slot, r0 : r0 + nr, c0 : c0 + nc]
        return carry

    lax.fori_loop(1, WIDE, fill, 0)
    frecv[w] = message[w]
    for c, (r0, nr, c0, nc, ring_z) in enumerate(BOXES):
        rbuf[c][w] = hbuf[slot_s[w], r0 : r0 + nr, c0 : c0 + nc]
    pl.semaphore_wait(barrier, PEERS + NARROW - 1)

    def send_facts(k, c):
        d = (w + k) % WIDE
        remote(message.at[d], frecv.at[w], factsem.at[0], factsem.at[1], (d, z)).start()
        return c

    lax.fori_loop(1, WIDE, send_facts, 0)
    for c in range(NBOX):

        def send_box(k, carry):
            d = (w + k) % WIDE
            remote(sbuf[c].at[k], rbuf[c].at[w], boxsend.at[c], boxrecv.at[c], (d, z)).start()
            return carry

        lax.fori_loop(1, WIDE, send_box, 0)
    all_facts = remote(
        message.at[pl.ds(0, PEERS)], frecv.at[pl.ds(0, PEERS)], factsem.at[0], factsem.at[1],
        ((w + 1) % WIDE, z),
    )
    all_facts.wait_recv()
    down = pltpu.make_async_copy(frecv, fsm, fsem)
    down.start()
    down.wait()

    def scan(s, carry):
        count, picks = carry
        live = fsm[s, 0, LIVE]
        place_s[s] = jnp.minimum(count, OWNED - 1)
        picks = tuple(jnp.where((live > 0) & (count == p), s, picks[p]) for p in range(OWNED))
        return count + live, picks

    _, picks = lax.fori_loop(
        0, WIDE, scan, (jnp.int32(0), tuple(jnp.int32(0) for _ in range(OWNED)))
    )
    for p in range(OWNED):
        pick_s[p] = picks[p]
        facts8[p : p + 1, :] = frecv[picks[p]]

    def known(p, which):
        return fsm[pick_s[p], 0, which]

    def hop(c, quarter, lo, size, to, n):
        r0, nr, c0, nc, _ = BOXES[c]
        where = crop.at[quarter, pl.ds(lo, size), pl.ds(r0, nr), pl.ds(c0, nc)]
        return remote(where, where, zsend.at[c, n], zrecv.at[c, n], (w, to))

    all_boxes = []
    z_sent = []

    def z_start(copy):
        copy.start()
        z_sent.append(copy)

    def pass_on(c):
        if BOXES[c][4]:
            hop(c, left, 0, OWNED, left, 0).wait_recv()
            z_start(hop(c, left, 0, part, right, 2))
            hop(c, right, 0, OWNED, right, 1).wait_recv()
            z_start(hop(c, right, part, part, left, 3))

    for c, (r0, nr, c0, nc, ring_z) in enumerate(BOXES):
        boxes = remote(
            sbuf[c].at[pl.ds(0, PEERS)], rbuf[c].at[pl.ds(0, PEERS)], boxsend.at[c],
            boxrecv.at[c], ((w + 1) % WIDE, z),
        )
        all_boxes.append(boxes)
        boxes.wait_recv()
        for p in range(OWNED):
            crop[z, p, r0 : r0 + nr, c0 : c0 + nc] = rbuf[c][picks[p]]
        if not ring_z:
            z_start(hop(c, z, 0, OWNED, opposite, 2))
        z_start(hop(c, z, 0, OWNED, right, 0))
        z_start(hop(c, z, 0, OWNED, left, 1))
        if c > 0:
            pass_on(c - 1)
    pass_on(NBOX - 1)
    for c, box in enumerate(BOXES):
        if box[4]:
            hop(c, opposite, 0, part, left, 2).wait_recv()
            hop(c, opposite, part, part, right, 3).wait_recv()
        else:
            hop(c, left, 0, OWNED, left, 0).wait_recv()
            hop(c, right, 0, OWNED, right, 1).wait_recv()
            hop(c, opposite, 0, OWNED, opposite, 2).wait_recv()

    diag = head_diag()
    ones = jnp.where(diag, 1.0, 0.0).astype(BF)
    row48 = iota((SPAN, QROWS), 0)
    col48 = iota((SPAN, QROWS), 1)
    for p in range(OWNED):
        start = known(p, START)
        length = known(p, LEN)
        rows = pl.ds(p * SPAN, SPAN)
        source = row48 + start
        alive = row48 < length
        top = jnp.where((col48 == source) & alive, 1.0, 0.0).astype(BF)
        low = jnp.where((col48 + QROWS == source) & alive, 1.0, 0.0).astype(BF)
        lhs = mm(top, crop[0, p]) + mm(low, crop[2, p])
        rhs = mm(top, crop[1, p]) + mm(low, crop[3, p])
        square = jnp.sum(lhs * lhs, axis=1, keepdims=True) + jnp.sum(
            rhs * rhs, axis=1, keepdims=True
        )
        inv = lax.rsqrt(square * (1.0 / D) + EPS)
        normed[rows, 0:QCOLS] = (lhs * inv).astype(BF)
        normed[rows, QCOLS:D] = (rhs * inv).astype(BF)
        inv_tokens[rows, :] = jnp.broadcast_to(inv, (SPAN, 128))
        scale = length.astype(F32)
        pooled[p : p + 1, 0:QCOLS] = jnp.sum(lhs, axis=0, keepdims=True) / scale
        pooled[p : p + 1, QCOLS:D] = jnp.sum(rhs, axis=0, keepdims=True) / scale
    load_qkv.wait()
    load_out.wait()
    for j in range(9):
        cols = pl.ds(j * GROUP, GROUP)
        mixed = mm(normed[...], wqkv[:, cols])
        if j < 6:
            square = mm((mixed * mixed).astype(BF), ones)
            inv = lax.rsqrt(square * (1.0 / HEAD) + EPS)
            qkv[:, cols] = (mixed * inv).astype(BF)
            inv_heads[:, cols] = inv.astype(BF)
        else:
            qkv[:, cols] = mixed.astype(BF)

    ones_lane = iota((1, GROUP), 1) % SPAN
    query_block = ones_lane // 16
    key_row = iota((SPAN, GROUP), 0)
    key_block = key_row // 16
    causal = key_row <= ones_lane

    def attend(p):
        rows = pl.ds(pl.multiple_of(p * SPAN, SPAN), SPAN)
        length = known(p, LEN)
        listed = None
        for j in range(4):
            want = [known(p, BLOCKS + 4 * b + j) for b in range(4)]
            want = jnp.where(
                query_block < 2,
                jnp.where(query_block == 0, want[0], want[1]),
                jnp.where(query_block == 2, want[2], want[3]),
            )
            hit = key_block == want
            listed = hit if listed is None else listed | hit
        allowed = jnp.where(listed & causal, 1.0, 0.0)
        alive = jnp.where(ones_lane < length, 1.0, 0.0)
        scale = length.astype(F32)
        for g in range(3):
            cols = pl.ds(g * GROUP, GROUP)
            query = spread_heads(qkv[rows, cols], diag)
            keys = qkv[rows, pl.ds(D + g * GROUP, GROUP)]
            weight = jnp.exp(mm_t(keys, query) * (4.0 / HEAD)) * allowed
            total = jnp.sum(weight, axis=0, keepdims=True)
            prob = (weight * (alive / total)).astype(BF)
            probs[p, :, cols] = prob
            column = mm(prob, ones) / scale
            col_w[rows, cols] = column
            values = qkv[rows, pl.ds(2 * D + g * GROUP, GROUP)].astype(F32)
            mean_att[pl.ds(p, 1), cols] = jnp.sum(column * values, axis=0, keepdims=True)

    def attend_some(i, carry):
        for q in range(PAIR):
            attend(i * PAIR + q)
        return carry

    lax.fori_loop(0, OWNED // PAIR, attend_some, 0)
    att_hi, att_lo = split_hi_lo(mean_att[...])
    pooled[...] += mm(att_hi, wout[...]) + mm(att_lo, wout[...])

    pool = pooled[...]
    inv_pool = lax.rsqrt(jnp.sum(pool * pool, axis=1, keepdims=True) + EPS)
    embed = pool * inv_pool
    mine[:, 0:D] = embed
    mine[:, D : D + 128] = jnp.broadcast_to(facts8[:, OFF : OFF + 1].astype(F32), (OWNED, 128))
    e_copies = []
    for k in range(1, NARROW):
        copy = remote(
            mine, everyone.at[z], esend.at[k], erecv.at[k], (w, (z + k) % NARROW)
        )
        copy.start()
        e_copies.append(copy)
    everyone[z] = mine[...]
    normed_t[...] = normed[...].T
    for k in range(1, NARROW):
        s = (z + NARROW - k) % NARROW
        remote(mine, everyone.at[s], esend.at[k], erecv.at[k], (w, s)).wait_recv()
    total = NARROW * OWNED
    full = everyone[...].reshape(total, D + 128)
    group = full[:, 0:D]
    offset = full[:, D : D + total].astype(I32)
    high = lax.Precision.HIGHEST
    logit = (
        lax.dot_general(
            group, group, (((1,), (1,)), ((), ())), precision=high, preferred_element_type=F32
        )
        / 0.1
    )
    row = iota((total, total), 0)
    col = iota((total, total), 1)
    positive = ((row // OWNED + offset) % NARROW) * OWNED + row % OWNED
    weight = jnp.where(row != col, jnp.exp(logit), 0.0)
    prob = weight / jnp.sum(weight, axis=1, keepdims=True)
    coef = (512.0 / 0.1) * (prob - jnp.where(col == positive, 1.0, 0.0))
    d_embed[...] = jnp.dot(
        coef, group, precision=high, preferred_element_type=F32
    ) + lax.dot_general(
        coef, group, (((0,), (0,)), ((), ())), precision=high, preferred_element_type=F32
    )
    own = d_embed[pl.ds(pl.multiple_of(OWNED * z, OWNED), OWNED), :]
    d_pooled[...] = inv_pool * (own - embed * jnp.sum(own * embed, axis=1, keepdims=True))

    hi, lo = split_hi_lo(d_pooled[...])
    d_att[...] = mm_t(hi, wout[...]) + mm_t(lo, wout[...])
    other = w + 1 - 2 * core
    w_sent = []

    def put_dw(t, j, got):
        dw[t, :, :, :, pl.ds(j * GROUP, GROUP)] = got.reshape(16, 2, WROWS, GROUP).astype(BF)

    def cross(t):
        return remote(dw.at[t, :, 1 - core], core_in.at[t], csend.at[t], crecv.at[t], (other, z))

    def along(t, first, k):
        if (t in (0, 3)) == first:
            return ((y * CHIP_X + (x + k) % CHIP_X) * 2 + core, z), (x + k) % CHIP_X
        return ((((y + k) % CHIP_Y) * CHIP_X + x) * 2 + core, z), (y + k) % CHIP_Y

    def start_cross(t):
        w_sent.append(cross(t))
        w_sent[-1].start()

    def start_first(t):
        cross(t).wait_recv()

        def pair(i, carry):
            at = (i % CHIP_X, i // CHIP_X) if t in (0, 3) else (i // CHIP_X, i % CHIP_X)
            acc[t, at[0], at[1]] = (
                dw[t, i, core].astype(F32) + core_in[t, i].astype(F32)
            ).astype(BF)
            return carry

        lax.fori_loop(0, CHIP_X * CHIP_Y, pair, 0)
        for k in (2, 1, 3):
            to, at = along(t, True, k)
            w_sent.append(
                remote(acc.at[t, at], ring.at[t, k], asend.at[t, k], arecv.at[t, k], to)
            )
            w_sent[-1].start()

    def start_second(t):
        for k in range(1, 4):
            to, at = along(t, True, k)
            remote(acc.at[t, at], ring.at[t, k], asend.at[t, k], arecv.at[t, k], to).wait_recv()
        here = along(t, True, 0)[1]

        def middle(i, carry):
            mid[t, i] = (
                (acc[t, here, i].astype(F32) + ring[t, 1, i].astype(F32))
                + (ring[t, 2, i].astype(F32) + ring[t, 3, i].astype(F32))
            ).astype(BF)
            return carry

        lax.fori_loop(0, 4, middle, 0)
        for k in (2, 1, 3):
            to, at = along(t, False, k)
            w_sent.append(
                remote(mid.at[t, at], ends.at[t, k], a2send.at[t, k], a2recv.at[t, k], to)
            )
            w_sent[-1].start()

    def finish_second(t):
        for k in range(1, 4):
            to, at = along(t, False, k)
            remote(mid.at[t, at], ends.at[t, k], a2send.at[t, k], a2recv.at[t, k], to).wait_recv()
        here = along(t, False, 0)[1]
        final[t, 0:WROWS, :] = (mid[t, here].astype(F32) + ends[t, 1].astype(F32)) + (
            ends[t, 2].astype(F32) + ends[t, 3].astype(F32)
        )
        final[t, WROWS : WROWS + 8, :] = jnp.zeros((8, D), F32)
        for j in range(NARROW):
            zbuf[t, j] = final[t, 6 * j : 6 * j + 8, :]
        for k in (2, 1, 3):
            d = (z + k) % NARROW
            w_sent.append(
                remote(zbuf.at[t, d], zlast.at[t, k], lsend.at[t, k], lrecv.at[t, k], (w, d))
            )
            w_sent[-1].start()

    def finish_last(t):
        for k in range(1, NARROW):
            d = (z + k) % NARROW
            remote(zbuf.at[t, d], zlast.at[t, k], lsend.at[t, k], lrecv.at[t, k], (w, d)).wait_recv()
        out_w[:, t * D : (t + 1) * D] = (zbuf[t, z] + zlast[t, 1]) + (zlast[t, 2] + zlast[t, 3])

    both = jnp.concatenate([att_hi, att_lo], axis=0)
    twice = jnp.concatenate([hi, hi], axis=0)
    for j in range(3):
        put_dw(3, j, mm_l(both, twice[:, j * GROUP : (j + 1) * GROUP]))
    start_cross(3)
    for p in range(OWNED):
        rows = pl.ds(p * SPAN, SPAN)
        g_mixed[rows, 2 * D : 3 * D] = (col_w[rows, :] * d_att[p : p + 1, :]).astype(BF)
    for j in range(3):
        put_dw(2, j, mm(normed_t[...], g_mixed[:, pl.ds(2 * D + j * GROUP, GROUP)]))
    start_cross(2)
    start_first(3)

    def attend_back(p):
        rows = pl.ds(pl.multiple_of(p * SPAN, SPAN), SPAN)
        scale = known(p, LEN).astype(F32)
        for g in range(3):
            cols = pl.ds(g * GROUP, GROUP)
            kcols = pl.ds(D + g * GROUP, GROUP)
            query = spread_heads(qkv[rows, cols], diag)
            keys = qkv[rows, kcols]
            values = qkv[rows, pl.ds(2 * D + g * GROUP, GROUP)].astype(F32)
            d_row = d_att[pl.ds(p, 1), cols] / scale
            slope = mm((values * d_row).astype(BF), ones)
            prob = probs[p, :, cols].astype(F32)
            tilted = prob * slope
            center = jnp.sum(tilted, axis=0, keepdims=True)
            d_score = ((tilted - prob * center) * (4.0 / HEAD)).astype(BF)
            g_mixed[rows, kcols] = mm(d_score, query).astype(BF)
            g_mixed[rows, cols] = gather_heads(mm_l(d_score, keys), diag).astype(BF)

    def attend_back_some(i, carry):
        for q in range(PAIR):
            attend_back(i * PAIR + q)
        return carry

    lax.fori_loop(0, 1, attend_back_some, 0)
    start_first(2)
    lax.fori_loop(1, 2, attend_back_some, 0)
    for j in range(6):
        cols = pl.ds(j * GROUP, GROUP)
        unit = qkv[:, cols].astype(F32)
        grad = g_mixed[:, cols].astype(F32)
        mean = mm((grad * unit).astype(BF), ones) * (1.0 / HEAD)
        g_mixed[:, cols] = (inv_heads[:, cols].astype(F32) * (grad - unit * mean)).astype(BF)
    for t in (0, 1):
        for j in range(3):
            put_dw(t, j, mm(normed_t[...], g_mixed[:, pl.ds(t * D + j * GROUP, GROUP)]))
        start_cross(t)
    for j in range(3):
        cols = pl.ds(j * GROUP, GROUP)
        d_normed[:, cols] = mm_t(g_mixed[...], wqkv[cols, :])
    start_first(0)
    start_first(1)
    for p in range(OWNED):
        rows = pl.ds(p * SPAN, SPAN)
        length = known(p, LEN)
        unit = normed[rows, :].astype(F32)
        grad = d_normed[rows, :]
        mean = jnp.sum(grad * unit, axis=1, keepdims=True) * (1.0 / D)
        back = inv_tokens[rows, 0:1] * (grad - unit * mean)
        back = back + d_pooled[p : p + 1, :] / length.astype(F32)
        alive = iota((SPAN, D), 0) < length
        d_tokens[rows, :] = jnp.where(alive, back, 0.0).astype(BF)

    h_sent = []

    def back_start(copy):
        copy.start()
        h_sent.append(copy)

    def h_direct(c, k, quarter, to):
        return remote(
            d_hist[c].at[quarter], zin[c].at[k], hsend.at[c, k], hrecv.at[c, k], (w, to)
        )

    def h_slot(c, slot):
        return zin[c].at[slot // 2, pl.ds(part * (slot % 2), part)]

    def h_step(c, quarter, lo, n, to):
        return remote(
            d_hist[c].at[quarter, pl.ds(lo, part)], h_slot(c, n), hsend.at[c, n],
            hrecv.at[c, n], (w, to),
        )

    def h_pass(c, side, to):
        return remote(
            comb[c].at[side], h_slot(c, 4 + side), hsend.at[c, 4 + side], hrecv.at[c, 4 + side],
            (w, to),
        )

    def h_relay(c):
        h_step(c, opposite, 0, 0, left).wait_recv()
        for p in range(part):
            comb[c][0, p] = (
                d_hist[c][right, p].astype(F32) + zin[c][0, p].astype(F32)
            ).astype(BF)
        back_start(h_pass(c, 0, right))
        h_step(c, opposite, part, 1, right).wait_recv()
        for p in range(part):
            comb[c][1, p] = (
                d_hist[c][left, part + p].astype(F32) + zin[c][0, part + p].astype(F32)
            ).astype(BF)
        back_start(h_pass(c, 1, left))

    def h_collect(c):
        if not BACKS[c][2]:
            for k in range(1, NARROW):
                s = (z + NARROW - k) % NARROW
                h_direct(c, k, s, s).wait_recv()
            for p in range(OWNED):
                dsum[c][p] = (
                    (d_hist[c][z, p].astype(F32) + zin[c][1, p].astype(F32))
                    + (zin[c][2, p].astype(F32) + zin[c][3, p].astype(F32))
                ).astype(BF)
            return
        h_step(c, right, part, 2, left).wait_recv()
        h_step(c, left, 0, 3, right).wait_recv()
        h_pass(c, 0, left).wait_recv()
        h_pass(c, 1, right).wait_recv()
        for p in range(part):
            dsum[c][p] = (
                (d_hist[c][z, p].astype(F32) + zin[c][2, p].astype(F32))
                + zin[c][1, part + p].astype(F32)
            ).astype(BF)
            dsum[c][part + p] = (
                (d_hist[c][z, part + p].astype(F32) + zin[c][2, part + p].astype(F32))
                + zin[c][1, p].astype(F32)
            ).astype(BF)

    shift = iota((HIST, SPAN), 0) - iota((HIST, SPAN), 1)
    puts = [jnp.where(shift == known(p, START), 1.0, 0.0).astype(BF) for p in range(OWNED)]
    for c, (c0, nc, ring_z) in enumerate(BACKS):
        for p in range(OWNED):
            spread = mm(puts[p], d_tokens[p * SPAN : (p + 1) * SPAN, c0 : c0 + nc])
            for j in range(NARROW):
                d_hist[c][j, p] = spread[j * ORROWS : (j + 1) * ORROWS].astype(BF)
        if ring_z:
            back_start(h_step(c, opposite, 0, 0, right))
            back_start(h_step(c, opposite, part, 1, left))
            back_start(h_step(c, right, part, 2, right))
            back_start(h_step(c, left, 0, 3, left))
        else:
            for k in (2, 1, 3):
                t = (z + k) % NARROW
                back_start(h_direct(c, k, t, t))
    start_second(3)
    start_second(2)
    all_back = []
    for c in range(NBACK):
        if BACKS[c][2]:
            h_relay(c)
    for c, (c0, nc, ring_z) in enumerate(BACKS):
        h_collect(c)

        def send_back(k, carry):
            d = (w + k) % WIDE
            sback[c][k] = dsum[c][place_s[d]]
            remote(sback[c].at[k], rback[c].at[w], backsend.at[c], backrecv.at[c], (d, z)).start()
            return carry

        lax.fori_loop(1, WIDE, send_back, 0)
        rback[c][w] = dsum[c][place_s[w]]
        all_back.append(
            remote(
                sback[c].at[pl.ds(0, PEERS)], rback[c].at[pl.ds(0, PEERS)], backsend.at[c],
                backrecv.at[c], ((w + 1) % WIDE, z),
            )
        )
        if c == 1:
            start_second(0)
            start_second(1)
    finish_second(3)
    finish_second(2)
    finish_second(0)
    finish_second(1)
    for c, (c0, nc, ring_z) in enumerate(BACKS):
        all_back[c].wait_recv()

        def write(a, carry):
            owner = dest[a]
            got = rback[c][jnp.maximum(owner, 0)].astype(F32)
            kept = jnp.where(jnp.full((ORROWS, nc), owner, I32) >= 0, got, 0.0)
            out_hist[a, :, c0 : c0 + nc] = kept.astype(BF)
            return carry

        lax.fori_loop(0, SLOTS, write, 0)
    for t in (3, 2, 0, 1):
        finish_last(t)

    all_facts.wait_send()
    for copy in all_boxes + z_sent + e_copies + w_sent + h_sent + all_back:
        copy.wait_send()


def finish_kernel(hist, d_w, out_hist, out_qkv, out_out):
    out_hist[...] = hist[...].astype(F32)
    out_qkv[...] = d_w[0:6, 0 : 3 * D]
    out_out[...] = d_w[0:6, 3 * D : WCOLS]


VM = pl.BlockSpec(memory_space=pltpu.VMEM)
SM = pl.BlockSpec(memory_space=pltpu.SMEM)
HB = pl.BlockSpec(memory_space=pl.ANY)
DMA = pltpu.SemaphoreType.DMA


def vmem(kind, *dims):
    return pltpu.VMEM(dims, kind)


def on_device(
    history, w_qkv, w_out, dest_owner, view_start, view_length, block_list, positive_offset
):
    d_history, d_w = pl.pallas_call(
        whole_kernel,
        out_shape=(
            jax.ShapeDtypeStruct((SLOTS, ORROWS, D), BF),
            jax.ShapeDtypeStruct((8, WCOLS), F32),
        ),
        in_specs=[SM, VM, VM, VM, VM, HB, HB, HB],
        out_specs=(VM, VM),
        scratch_shapes=[
            vmem(BF, D, 3 * D),
            vmem(BF, D, D),
            vmem(I32, 128, 128),
            vmem(I32, 128, 128),
            pltpu.SMEM((WIDE,), I32),
            vmem(I32, WIDE, 1, 128),
            vmem(I32, WIDE, 1, 128),
            pltpu.SMEM((WIDE, 1, 128), I32),
            pltpu.SMEM((OWNED,), I32),
            pltpu.SMEM((WIDE,), I32),
            vmem(I32, OWNED, 128),
            vmem(BF, SLOTS, QROWS, QCOLS),
            vmem(BF, NARROW, OWNED, QROWS, QCOLS),
            vmem(BF, ROWS, D),
            vmem(BF, D, ROWS),
            vmem(BF, ROWS, 3 * D),
            vmem(BF, ROWS, 2 * D),
            vmem(F32, ROWS, 128),
            vmem(BF, OWNED, SPAN, D),
            vmem(F32, ROWS, D),
            vmem(F32, OWNED, D),
            vmem(F32, OWNED, D),
            vmem(F32, OWNED, D + 128),
            vmem(F32, NARROW, OWNED, D + 128),
            vmem(F32, NARROW * OWNED, D),
            vmem(F32, OWNED, D),
            vmem(F32, OWNED, D),
            vmem(BF, ROWS, 3 * D),
            vmem(F32, ROWS, D),
            vmem(BF, ROWS, D),
            vmem(BF, 4, 16, 2, WROWS, D),
            vmem(BF, 4, 16, WROWS, D),
            vmem(BF, 4, 4, 4, WROWS, D),
            vmem(BF, 4, 4, 4, WROWS, D),
            vmem(BF, 4, 4, WROWS, D),
            vmem(BF, 4, 4, WROWS, D),
            vmem(F32, 4, WROWS + 8, D),
            vmem(F32, 4, NARROW, 8, D),
            vmem(F32, 4, NARROW, 8, D),
            *[vmem(BF, WIDE, nr, nc) for _, nr, _, nc, _ in BOXES],
            *[vmem(BF, WIDE, nr, nc) for _, nr, _, nc, _ in BOXES],
            *[vmem(BF, NARROW, OWNED, ORROWS, nc) for _, nc, _ in BACKS],
            *[vmem(BF, NARROW, OWNED, ORROWS, nc) for _, nc, _ in BACKS],
            *[vmem(BF, 2, OWNED // 2, ORROWS, nc) for _, nc, _ in BACKS],
            *[vmem(BF, OWNED, ORROWS, nc) for _, nc, _ in BACKS],
            *[vmem(BF, WIDE, ORROWS, nc) for _, nc, _ in BACKS],
            *[vmem(BF, WIDE, ORROWS, nc) for _, nc, _ in BACKS],
            DMA((2,)), DMA, DMA, DMA((2,)),
            DMA((NBOX,)), DMA((NBOX,)),
            DMA((NBOX, 4)), DMA((NBOX, 4)),
            DMA((NARROW,)), DMA((NARROW,)),
            DMA((4,)), DMA((4,)),
            DMA((4, 4)), DMA((4, 4)),
            DMA((4, 4)), DMA((4, 4)),
            DMA((4, 4)), DMA((4, 4)),
            DMA((NBACK, 6)), DMA((NBACK, 6)),
            DMA((NBACK,)), DMA((NBACK,)),
        ],
        compiler_params=pltpu.CompilerParams(
            collective_id=0, has_side_effects=True, vmem_limit_bytes=VMEM_LIMIT
        ),
        name="step",
    )(
        dest_owner, view_start.T, view_length.T, positive_offset.T,
        block_list.reshape(SLOTS, 16).T, history, w_qkv, w_out,
    )
    return pl.pallas_call(
        finish_kernel,
        out_shape=(
            jax.ShapeDtypeStruct((SLOTS, ORROWS, D), F32),
            jax.ShapeDtypeStruct((6, 3 * D), F32),
            jax.ShapeDtypeStruct((6, D), F32),
        ),
        in_specs=[VM, VM],
        out_specs=(VM, VM, VM),
        name="finish",
    )(d_history, d_w)


def solution(mesh):
    return jax.shard_map(
        on_device,
        mesh=mesh,
        in_specs=(
            P("wide", None, None),
            P(),
            P(),
            P("wide"),
            P("wide", "narrow"),
            P("wide", "narrow"),
            P("wide", "narrow", None, None),
            P("wide", "narrow"),
        ),
        out_specs=(
            P("wide", "narrow", None),
            P(("wide", "narrow"), None),
            P(("wide", "narrow"), None),
        ),
        check_vma=False,
    )
```

```python
import jax
import jax.numpy as jnp
from jax import lax
from jax.experimental import pallas as pl
from jax.experimental.pallas import tpu as pltpu
from jax.sharding import PartitionSpec as P

BF = jnp.bfloat16
F32 = jnp.float32
I32 = jnp.int32
MESH = pl.DeviceIdType.MESH

WIDE = 32
NARROW = 4
CHIP_X = 4
CHIP_Y = 4
OWNED = 8
SLOTS = 16
D = 768
HEAD = 64
SPAN = 64
HIST = 96
GROUP = 256
ROWS = OWNED * SPAN
QROWS = HIST // 2
QCOLS = D // 2
ORROWS = HIST // NARROW
WROWS = D // WIDE
WCOLS = 4 * D

LIVE, LEN, OFF, START, BLOCKS = 0, 1, 2, 3, 8
BOXES = (
    (0, 16, 0, 128, False),
    (0, 16, 128, 256, False),
    (16, 16, 0, 384, True),
    (32, 16, 0, 256, True),
    (32, 16, 256, 128, False),
)
NBOX = len(BOXES)
BACKS = ((0, 128, False), (128, 256, False), (384, 256, False), (640, 128, False))
NBACK = len(BACKS)
PAIR = 4
PEERS = WIDE - 1
EPS = 1e-06
VMEM_LIMIT = 60 * 1024 * 1024


def mm(a, b):
    return jnp.dot(a, b, preferred_element_type=F32)


def mm_t(a, b):
    return lax.dot_general(a, b, (((1,), (1,)), ((), ())), preferred_element_type=F32)


def mm_l(a, b):
    return lax.dot_general(a, b, (((0,), (0,)), ((), ())), preferred_element_type=F32)


def split_hi_lo(x):
    hi = x.astype(BF)
    return hi, (x - hi.astype(F32)).astype(BF)


def iota(shape, dim):
    return lax.broadcasted_iota(I32, shape, dim)


def head_diag():
    shape = (GROUP, GROUP)
    return (iota(shape, 0) // HEAD) == (iota(shape, 1) // HEAD)


def spread_heads(x, diag):
    return jnp.where(diag, jnp.concatenate([x, x, x, x], axis=0), jnp.zeros((), x.dtype))


def gather_heads(full, diag):
    kept = jnp.where(diag, full, 0.0)
    return (kept[0:64] + kept[64:128]) + (kept[128:192] + kept[192:256])


def whole_kernel(
    dest, starts, lengths, offsets, lists, hist, wqkv_hbm, wout_hbm,
    out_hist, out_w,
    wqkv, wout, fact_t, fact, slot_s, message, frecv, fsm, pick_s, place_s, facts8,
    hbuf, crop,
    normed, normed_t, qkv, inv_heads, inv_tokens, probs, col_w, pooled, mean_att,
    mine, everyone, d_embed, d_pooled, d_att, g_mixed, d_normed, d_tokens,
    dw, core_in, acc, ring, mid, ends, final, zbuf, zlast,
    sbuf_0, sbuf_1, sbuf_2, sbuf_3, sbuf_4, rbuf_0, rbuf_1, rbuf_2, rbuf_3, rbuf_4,
    hist_0, hist_1, hist_2, hist_3, zin_0, zin_1, zin_2, zin_3, comb_0, comb_1, comb_2, comb_3,
    dsum_0, dsum_1, dsum_2, dsum_3, sback_0, sback_1, sback_2, sback_3,
    rback_0, rback_1, rback_2, rback_3,
    wsem, lsem, fsem, factsem, boxsend, boxrecv, zsend, zrecv, esend, erecv,
    csend, crecv, asend, arecv, a2send, a2recv, lsend, lrecv,
    hsend, hrecv, backsend, backrecv,
):
    w = lax.axis_index("wide")
    z = lax.axis_index("narrow")
    core = w % 2
    x = (w // 2) % CHIP_X
    y = w // (2 * CHIP_X)
    def remote(src, dst, send, recv, to):
        return pltpu.make_async_remote_copy(
            src_ref=src, dst_ref=dst, send_sem=send, recv_sem=recv, device_id=to,
            device_id_type=MESH,
        )

    sbuf = (sbuf_0, sbuf_1, sbuf_2, sbuf_3, sbuf_4)
    rbuf = (rbuf_0, rbuf_1, rbuf_2, rbuf_3, rbuf_4)
    d_hist = (hist_0, hist_1, hist_2, hist_3)
    zin = (zin_0, zin_1, zin_2, zin_3)
    comb = (comb_0, comb_1, comb_2, comb_3)
    right = (z + 1) % NARROW
    left = (z + 3) % NARROW
    opposite = (z + 2) % NARROW
    part = OWNED // 2
    dsum = (dsum_0, dsum_1, dsum_2, dsum_3)
    sback = (sback_0, sback_1, sback_2, sback_3)
    rback = (rback_0, rback_1, rback_2, rback_3)

    load = pltpu.make_async_copy(
        hist.at[:, pl.ds(QROWS * (z // 2), QROWS), pl.ds(QCOLS * (z % 2), QCOLS)], hbuf, lsem
    )
    load.start()
    barrier = pltpu.get_barrier_semaphore()

    def greet(k, c):
        pl.semaphore_signal(barrier, inc=1, device_id=((w + k) % WIDE, z), device_id_type=MESH)
        return c

    lax.fori_loop(1, WIDE, greet, 0)
    for k in range(1, NARROW):
        pl.semaphore_signal(barrier, inc=1, device_id=(w, (z + k) % NARROW), device_id_type=MESH)
    load_qkv = pltpu.make_async_copy(wqkv_hbm, wqkv, wsem.at[0])
    load_out = pltpu.make_async_copy(wout_hbm, wout, wsem.at[1])
    load_qkv.start()
    load_out.start()

    fact_t[...] = jnp.zeros((128, 128), I32)
    fact_t[LIVE : LIVE + 1, :] = jnp.ones((1, 128), I32)
    fact_t[LEN : LEN + 1, 0:SLOTS] = lengths[...]
    fact_t[OFF : OFF + 1, 0:SLOTS] = offsets[...]
    fact_t[START : START + 1, 0:SLOTS] = starts[...]
    fact_t[BLOCKS : BLOCKS + 16, 0:SLOTS] = lists[...]
    fact[...] = fact_t[...].T
    owners = [dest[a] for a in range(SLOTS)]

    def find(d, c):
        slot = jnp.int32(0)
        live = jnp.int32(0)
        for a in range(SLOTS):
            hit = owners[a] == d
            slot = jnp.where(hit, a, slot)
            live = jnp.where(hit, 1, live)
        slot_s[d] = slot
        message[d] = fact[pl.ds(slot, 1), :] * live
        return c

    lax.fori_loop(0, WIDE, find, 0)
    load.wait()

    def fill(k, carry):
        slot = slot_s[(w + k) % WIDE]
        for c, (r0, nr, c0, nc, ring_z) in enumerate(BOXES):
            sbuf[c][k] = hbuf[slot, r0 : r0 + nr, c0 : c0 + nc]
        return carry

    lax.fori_loop(1, WIDE, fill, 0)
    frecv[w] = message[w]
    for c, (r0, nr, c0, nc, ring_z) in enumerate(BOXES):
        rbuf[c][w] = hbuf[slot_s[w], r0 : r0 + nr, c0 : c0 + nc]
    pl.semaphore_wait(barrier, PEERS + NARROW - 1)

    def send_facts(k, c):
        d = (w + k) % WIDE
        remote(message.at[d], frecv.at[w], factsem.at[0], factsem.at[1], (d, z)).start()
        return c

    lax.fori_loop(1, WIDE, send_facts, 0)
    for c in range(NBOX):

        def send_box(k, carry):
            d = (w + k) % WIDE
            remote(sbuf[c].at[k], rbuf[c].at[w], boxsend.at[c], boxrecv.at[c], (d, z)).start()
            return carry

        lax.fori_loop(1, WIDE, send_box, 0)
    all_facts = remote(
        message.at[pl.ds(0, PEERS)], frecv.at[pl.ds(0, PEERS)], factsem.at[0], factsem.at[1],
        ((w + 1) % WIDE, z),
    )
    all_facts.wait_recv()
    down = pltpu.make_async_copy(frecv, fsm, fsem)
    down.start()
    down.wait()

    def scan(s, carry):
        count, picks = carry
        live = fsm[s, 0, LIVE]
        place_s[s] = jnp.minimum(count, OWNED - 1)
        picks = tuple(jnp.where((live > 0) & (count == p), s, picks[p]) for p in range(OWNED))
        return count + live, picks

    _, picks = lax.fori_loop(
        0, WIDE, scan, (jnp.int32(0), tuple(jnp.int32(0) for _ in range(OWNED)))
    )
    for p in range(OWNED):
        pick_s[p] = picks[p]
        facts8[p : p + 1, :] = frecv[picks[p]]

    def known(p, which):
        return fsm[pick_s[p], 0, which]

    def hop(c, quarter, lo, size, to, n):
        r0, nr, c0, nc, _ = BOXES[c]
        where = crop.at[quarter, pl.ds(lo, size), pl.ds(r0, nr), pl.ds(c0, nc)]
        return remote(where, where, zsend.at[c, n], zrecv.at[c, n], (w, to))

    all_boxes = []
    z_sent = []

    def z_start(copy):
        copy.start()
        z_sent.append(copy)

    def pass_on(c):
        if BOXES[c][4]:
            hop(c, left, 0, OWNED, left, 0).wait_recv()
            z_start(hop(c, left, 0, part, right, 2))
            hop(c, right, 0, OWNED, right, 1).wait_recv()
            z_start(hop(c, right, part, part, left, 3))

    for c, (r0, nr, c0, nc, ring_z) in enumerate(BOXES):
        boxes = remote(
            sbuf[c].at[pl.ds(0, PEERS)], rbuf[c].at[pl.ds(0, PEERS)], boxsend.at[c],
            boxrecv.at[c], ((w + 1) % WIDE, z),
        )
        all_boxes.append(boxes)
        boxes.wait_recv()
        for p in range(OWNED):
            crop[z, p, r0 : r0 + nr, c0 : c0 + nc] = rbuf[c][picks[p]]
        if not ring_z:
            z_start(hop(c, z, 0, OWNED, opposite, 2))
        z_start(hop(c, z, 0, OWNED, right, 0))
        z_start(hop(c, z, 0, OWNED, left, 1))
        if c > 0:
            pass_on(c - 1)
    pass_on(NBOX - 1)
    for c, box in enumerate(BOXES):
        if box[4]:
            hop(c, opposite, 0, part, left, 2).wait_recv()
            hop(c, opposite, part, part, right, 3).wait_recv()
        else:
            hop(c, left, 0, OWNED, left, 0).wait_recv()
            hop(c, right, 0, OWNED, right, 1).wait_recv()
            hop(c, opposite, 0, OWNED, opposite, 2).wait_recv()

    diag = head_diag()
    ones = jnp.where(diag, 1.0, 0.0).astype(BF)
    row48 = iota((SPAN, QROWS), 0)
    col48 = iota((SPAN, QROWS), 1)
    for p in range(OWNED):
        start = known(p, START)
        length = known(p, LEN)
        rows = pl.ds(p * SPAN, SPAN)
        source = row48 + start
        alive = row48 < length
        top = jnp.where((col48 == source) & alive, 1.0, 0.0).astype(BF)
        low = jnp.where((col48 + QROWS == source) & alive, 1.0, 0.0).astype(BF)
        lhs = mm(top, crop[0, p]) + mm(low, crop[2, p])
        rhs = mm(top, crop[1, p]) + mm(low, crop[3, p])
        square = jnp.sum(lhs * lhs, axis=1, keepdims=True) + jnp.sum(
            rhs * rhs, axis=1, keepdims=True
        )
        inv = lax.rsqrt(square * (1.0 / D) + EPS)
        normed[rows, 0:QCOLS] = (lhs * inv).astype(BF)
        normed[rows, QCOLS:D] = (rhs * inv).astype(BF)
        inv_tokens[rows, :] = jnp.broadcast_to(inv, (SPAN, 128))
        scale = length.astype(F32)
        pooled[p : p + 1, 0:QCOLS] = jnp.sum(lhs, axis=0, keepdims=True) / scale
        pooled[p : p + 1, QCOLS:D] = jnp.sum(rhs, axis=0, keepdims=True) / scale
    load_qkv.wait()
    load_out.wait()
    for j in range(9):
        cols = pl.ds(j * GROUP, GROUP)
        mixed = mm(normed[...], wqkv[:, cols])
        if j < 6:
            square = mm((mixed * mixed).astype(BF), ones)
            inv = lax.rsqrt(square * (1.0 / HEAD) + EPS)
            qkv[:, cols] = (mixed * inv).astype(BF)
            inv_heads[:, cols] = inv.astype(BF)
        else:
            qkv[:, cols] = mixed.astype(BF)

    ones_lane = iota((1, GROUP), 1) % SPAN
    query_block = ones_lane // 16
    key_row = iota((SPAN, GROUP), 0)
    key_block = key_row // 16
    causal = key_row <= ones_lane

    def attend(p):
        rows = pl.ds(pl.multiple_of(p * SPAN, SPAN), SPAN)
        length = known(p, LEN)
        listed = None
        for j in range(4):
            want = [known(p, BLOCKS + 4 * b + j) for b in range(4)]
            want = jnp.where(
                query_block < 2,
                jnp.where(query_block == 0, want[0], want[1]),
                jnp.where(query_block == 2, want[2], want[3]),
            )
            hit = key_block == want
            listed = hit if listed is None else listed | hit
        allowed = jnp.where(listed & causal, 1.0, 0.0)
        alive = jnp.where(ones_lane < length, 1.0, 0.0)
        scale = length.astype(F32)
        for g in range(3):
            cols = pl.ds(g * GROUP, GROUP)
            query = spread_heads(qkv[rows, cols], diag)
            keys = qkv[rows, pl.ds(D + g * GROUP, GROUP)]
            weight = jnp.exp(mm_t(keys, query) * (4.0 / HEAD)) * allowed
            total = jnp.sum(weight, axis=0, keepdims=True)
            prob = (weight * (alive / total)).astype(BF)
            probs[p, :, cols] = prob
            column = mm(prob, ones) / scale
            col_w[rows, cols] = column
            values = qkv[rows, pl.ds(2 * D + g * GROUP, GROUP)].astype(F32)
            mean_att[pl.ds(p, 1), cols] = jnp.sum(column * values, axis=0, keepdims=True)

    def attend_some(i, carry):
        for q in range(PAIR):
            attend(i * PAIR + q)
        return carry

    lax.fori_loop(0, OWNED // PAIR, attend_some, 0)
    att_hi, att_lo = split_hi_lo(mean_att[...])
    pooled[...] += mm(att_hi, wout[...]) + mm(att_lo, wout[...])

    pool = pooled[...]
    inv_pool = lax.rsqrt(jnp.sum(pool * pool, axis=1, keepdims=True) + EPS)
    embed = pool * inv_pool
    mine[:, 0:D] = embed
    mine[:, D : D + 128] = jnp.broadcast_to(facts8[:, OFF : OFF + 1].astype(F32), (OWNED, 128))
    e_copies = []
    for k in range(1, NARROW):
        copy = remote(
            mine, everyone.at[z], esend.at[k], erecv.at[k], (w, (z + k) % NARROW)
        )
        copy.start()
        e_copies.append(copy)
    everyone[z] = mine[...]
    normed_t[...] = normed[...].T
    for k in range(1, NARROW):
        s = (z + NARROW - k) % NARROW
        remote(mine, everyone.at[s], esend.at[k], erecv.at[k], (w, s)).wait_recv()
    total = NARROW * OWNED
    full = everyone[...].reshape(total, D + 128)
    group = full[:, 0:D]
    offset = full[:, D : D + total].astype(I32)
    high = lax.Precision.HIGHEST
    logit = (
        lax.dot_general(
            group, group, (((1,), (1,)), ((), ())), precision=high, preferred_element_type=F32
        )
        / 0.1
    )
    row = iota((total, total), 0)
    col = iota((total, total), 1)
    positive = ((row // OWNED + offset) % NARROW) * OWNED + row % OWNED
    weight = jnp.where(row != col, jnp.exp(logit), 0.0)
    prob = weight / jnp.sum(weight, axis=1, keepdims=True)
    coef = (512.0 / 0.1) * (prob - jnp.where(col == positive, 1.0, 0.0))
    d_embed[...] = jnp.dot(
        coef, group, precision=high, preferred_element_type=F32
    ) + lax.dot_general(
        coef, group, (((0,), (0,)), ((), ())), precision=high, preferred_element_type=F32
    )
    own = d_embed[pl.ds(pl.multiple_of(OWNED * z, OWNED), OWNED), :]
    d_pooled[...] = inv_pool * (own - embed * jnp.sum(own * embed, axis=1, keepdims=True))

    hi, lo = split_hi_lo(d_pooled[...])
    d_att[...] = mm_t(hi, wout[...]) + mm_t(lo, wout[...])
    other = w + 1 - 2 * core
    w_sent = []

    def put_dw(t, j, got):
        dw[t, :, :, :, pl.ds(j * GROUP, GROUP)] = got.reshape(16, 2, WROWS, GROUP).astype(BF)

    def cross(t):
        return remote(dw.at[t, :, 1 - core], core_in.at[t], csend.at[t], crecv.at[t], (other, z))

    def along(t, first, k):
        if (t in (0, 3)) == first:
            return ((y * CHIP_X + (x + k) % CHIP_X) * 2 + core, z), (x + k) % CHIP_X
        return ((((y + k) % CHIP_Y) * CHIP_X + x) * 2 + core, z), (y + k) % CHIP_Y

    def start_cross(t):
        w_sent.append(cross(t))
        w_sent[-1].start()

    def start_first(t):
        cross(t).wait_recv()

        def pair(i, carry):
            at = (i % CHIP_X, i // CHIP_X) if t in (0, 3) else (i // CHIP_X, i % CHIP_X)
            acc[t, at[0], at[1]] = (
                dw[t, i, core].astype(F32) + core_in[t, i].astype(F32)
            ).astype(BF)
            return carry

        lax.fori_loop(0, CHIP_X * CHIP_Y, pair, 0)
        for k in (2, 1, 3):
            to, at = along(t, True, k)
            w_sent.append(
                remote(acc.at[t, at], ring.at[t, k], asend.at[t, k], arecv.at[t, k], to)
            )
            w_sent[-1].start()

    def start_second(t):
        for k in range(1, 4):
            to, at = along(t, True, k)
            remote(acc.at[t, at], ring.at[t, k], asend.at[t, k], arecv.at[t, k], to).wait_recv()
        here = along(t, True, 0)[1]

        def middle(i, carry):
            mid[t, i] = (
                (acc[t, here, i].astype(F32) + ring[t, 1, i].astype(F32))
                + (ring[t, 2, i].astype(F32) + ring[t, 3, i].astype(F32))
            ).astype(BF)
            return carry

        lax.fori_loop(0, 4, middle, 0)
        for k in (2, 1, 3):
            to, at = along(t, False, k)
            w_sent.append(
                remote(mid.at[t, at], ends.at[t, k], a2send.at[t, k], a2recv.at[t, k], to)
            )
            w_sent[-1].start()

    def finish_second(t):
        for k in range(1, 4):
            to, at = along(t, False, k)
            remote(mid.at[t, at], ends.at[t, k], a2send.at[t, k], a2recv.at[t, k], to).wait_recv()
        here = along(t, False, 0)[1]
        final[t, 0:WROWS, :] = (mid[t, here].astype(F32) + ends[t, 1].astype(F32)) + (
            ends[t, 2].astype(F32) + ends[t, 3].astype(F32)
        )
        final[t, WROWS : WROWS + 8, :] = jnp.zeros((8, D), F32)
        for j in range(NARROW):
            zbuf[t, j] = final[t, 6 * j : 6 * j + 8, :]
        for k in (2, 1, 3):
            d = (z + k) % NARROW
            w_sent.append(
                remote(zbuf.at[t, d], zlast.at[t, k], lsend.at[t, k], lrecv.at[t, k], (w, d))
            )
            w_sent[-1].start()

    def finish_last(t):
        for k in range(1, NARROW):
            d = (z + k) % NARROW
            remote(zbuf.at[t, d], zlast.at[t, k], lsend.at[t, k], lrecv.at[t, k], (w, d)).wait_recv()
        out_w[:, t * D : (t + 1) * D] = (zbuf[t, z] + zlast[t, 1]) + (zlast[t, 2] + zlast[t, 3])

    both = jnp.concatenate([att_hi, att_lo], axis=0)
    twice = jnp.concatenate([hi, hi], axis=0)
    for j in range(3):
        put_dw(3, j, mm_l(both, twice[:, j * GROUP : (j + 1) * GROUP]))
    start_cross(3)
    for p in range(OWNED):
        rows = pl.ds(p * SPAN, SPAN)
        g_mixed[rows, 2 * D : 3 * D] = (col_w[rows, :] * d_att[p : p + 1, :]).astype(BF)
    for j in range(3):
        put_dw(2, j, mm(normed_t[...], g_mixed[:, pl.ds(2 * D + j * GROUP, GROUP)]))
    start_cross(2)
    start_first(3)

    def attend_back(p):
        rows = pl.ds(pl.multiple_of(p * SPAN, SPAN), SPAN)
        scale = known(p, LEN).astype(F32)
        for g in range(3):
            cols = pl.ds(g * GROUP, GROUP)
            kcols = pl.ds(D + g * GROUP, GROUP)
            query = spread_heads(qkv[rows, cols], diag)
            keys = qkv[rows, kcols]
            values = qkv[rows, pl.ds(2 * D + g * GROUP, GROUP)].astype(F32)
            d_row = d_att[pl.ds(p, 1), cols] / scale
            slope = mm((values * d_row).astype(BF), ones)
            prob = probs[p, :, cols].astype(F32)
            tilted = prob * slope
            center = jnp.sum(tilted, axis=0, keepdims=True)
            d_score = ((tilted - prob * center) * (4.0 / HEAD)).astype(BF)
            g_mixed[rows, kcols] = mm(d_score, query).astype(BF)
            g_mixed[rows, cols] = gather_heads(mm_l(d_score, keys), diag).astype(BF)

    def attend_back_some(i, carry):
        for q in range(PAIR):
            attend_back(i * PAIR + q)
        return carry

    lax.fori_loop(0, 1, attend_back_some, 0)
    start_first(2)
    lax.fori_loop(1, 2, attend_back_some, 0)
    for j in range(6):
        cols = pl.ds(j * GROUP, GROUP)
        unit = qkv[:, cols].astype(F32)
        grad = g_mixed[:, cols].astype(F32)
        mean = mm((grad * unit).astype(BF), ones) * (1.0 / HEAD)
        g_mixed[:, cols] = (inv_heads[:, cols].astype(F32) * (grad - unit * mean)).astype(BF)
    for t in (0, 1):
        for j in range(3):
            put_dw(t, j, mm(normed_t[...], g_mixed[:, pl.ds(t * D + j * GROUP, GROUP)]))
        start_cross(t)
    for j in range(3):
        cols = pl.ds(j * GROUP, GROUP)
        d_normed[:, cols] = mm_t(g_mixed[...], wqkv[cols, :])
    start_first(0)
    start_first(1)
    for p in range(OWNED):
        rows = pl.ds(p * SPAN, SPAN)
        length = known(p, LEN)
        unit = normed[rows, :].astype(F32)
        grad = d_normed[rows, :]
        mean = jnp.sum(grad * unit, axis=1, keepdims=True) * (1.0 / D)
        back = inv_tokens[rows, 0:1] * (grad - unit * mean)
        back = back + d_pooled[p : p + 1, :] / length.astype(F32)
        alive = iota((SPAN, D), 0) < length
        d_tokens[rows, :] = jnp.where(alive, back, 0.0).astype(BF)

    h_sent = []

    def back_start(copy):
        copy.start()
        h_sent.append(copy)

    def h_direct(c, k, quarter, to):
        return remote(
            d_hist[c].at[quarter], zin[c].at[k], hsend.at[c, k], hrecv.at[c, k], (w, to)
        )

    def h_slot(c, slot):
        return zin[c].at[slot // 2, pl.ds(part * (slot % 2), part)]

    def h_step(c, quarter, lo, n, to):
        return remote(
            d_hist[c].at[quarter, pl.ds(lo, part)], h_slot(c, n), hsend.at[c, n],
            hrecv.at[c, n], (w, to),
        )

    def h_pass(c, side, to):
        return remote(
            comb[c].at[side], h_slot(c, 4 + side), hsend.at[c, 4 + side], hrecv.at[c, 4 + side],
            (w, to),
        )

    def h_relay(c):
        h_step(c, opposite, 0, 0, left).wait_recv()
        for p in range(part):
            comb[c][0, p] = (
                d_hist[c][right, p].astype(F32) + zin[c][0, p].astype(F32)
            ).astype(BF)
        back_start(h_pass(c, 0, right))
        h_step(c, opposite, part, 1, right).wait_recv()
        for p in range(part):
            comb[c][1, p] = (
                d_hist[c][left, part + p].astype(F32) + zin[c][0, part + p].astype(F32)
            ).astype(BF)
        back_start(h_pass(c, 1, left))

    def h_collect(c):
        if not BACKS[c][2]:
            for k in range(1, NARROW):
                s = (z + NARROW - k) % NARROW
                h_direct(c, k, s, s).wait_recv()
            for p in range(OWNED):
                dsum[c][p] = (
                    (d_hist[c][z, p].astype(F32) + zin[c][1, p].astype(F32))
                    + (zin[c][2, p].astype(F32) + zin[c][3, p].astype(F32))
                ).astype(BF)
            return
        h_step(c, right, part, 2, left).wait_recv()
        h_step(c, left, 0, 3, right).wait_recv()
        h_pass(c, 0, left).wait_recv()
        h_pass(c, 1, right).wait_recv()
        for p in range(part):
            dsum[c][p] = (
                (d_hist[c][z, p].astype(F32) + zin[c][2, p].astype(F32))
                + zin[c][1, part + p].astype(F32)
            ).astype(BF)
            dsum[c][part + p] = (
                (d_hist[c][z, part + p].astype(F32) + zin[c][2, part + p].astype(F32))
                + zin[c][1, p].astype(F32)
            ).astype(BF)

    shift = iota((HIST, SPAN), 0) - iota((HIST, SPAN), 1)
    puts = [jnp.where(shift == known(p, START), 1.0, 0.0).astype(BF) for p in range(OWNED)]
    for c, (c0, nc, ring_z) in enumerate(BACKS):
        for p in range(OWNED):
            spread = mm(puts[p], d_tokens[p * SPAN : (p + 1) * SPAN, c0 : c0 + nc])
            for j in range(NARROW):
                d_hist[c][j, p] = spread[j * ORROWS : (j + 1) * ORROWS].astype(BF)
        if ring_z:
            back_start(h_step(c, opposite, 0, 0, right))
            back_start(h_step(c, opposite, part, 1, left))
            back_start(h_step(c, right, part, 2, right))
            back_start(h_step(c, left, 0, 3, left))
        else:
            for k in (2, 1, 3):
                t = (z + k) % NARROW
                back_start(h_direct(c, k, t, t))
    start_second(3)
    start_second(2)
    all_back = []
    for c in range(NBACK):
        if BACKS[c][2]:
            h_relay(c)
    for c, (c0, nc, ring_z) in enumerate(BACKS):
        h_collect(c)

        def send_back(k, carry):
            d = (w + k) % WIDE
            sback[c][k] = dsum[c][place_s[d]]
            remote(sback[c].at[k], rback[c].at[w], backsend.at[c], backrecv.at[c], (d, z)).start()
            return carry

        lax.fori_loop(1, WIDE, send_back, 0)
        rback[c][w] = dsum[c][place_s[w]]
        all_back.append(
            remote(
                sback[c].at[pl.ds(0, PEERS)], rback[c].at[pl.ds(0, PEERS)], backsend.at[c],
                backrecv.at[c], ((w + 1) % WIDE, z),
            )
        )
        if c == 1:
            start_second(0)
            start_second(1)
    finish_second(3)
    finish_second(2)
    for c, (c0, nc, ring_z) in enumerate(BACKS):
        if c == 2:
            finish_second(0)
            finish_second(1)
        all_back[c].wait_recv()

        def write(a, carry):
            owner = dest[a]
            got = rback[c][jnp.maximum(owner, 0)].astype(F32)
            kept = jnp.where(jnp.full((ORROWS, nc), owner, I32) >= 0, got, 0.0)
            out_hist[a, :, c0 : c0 + nc] = kept.astype(BF)
            return carry

        lax.fori_loop(0, SLOTS, write, 0)
    for t in (3, 2, 0, 1):
        finish_last(t)

    all_facts.wait_send()
    for copy in all_boxes + z_sent + e_copies + w_sent + h_sent + all_back:
        copy.wait_send()


def finish_kernel(hist, d_w, out_hist, out_qkv, out_out):
    out_hist[...] = hist[...].astype(F32)
    out_qkv[...] = d_w[0:6, 0 : 3 * D]
    out_out[...] = d_w[0:6, 3 * D : WCOLS]


VM = pl.BlockSpec(memory_space=pltpu.VMEM)
SM = pl.BlockSpec(memory_space=pltpu.SMEM)
HB = pl.BlockSpec(memory_space=pl.ANY)
DMA = pltpu.SemaphoreType.DMA


def vmem(kind, *dims):
    return pltpu.VMEM(dims, kind)


def on_device(
    history, w_qkv, w_out, dest_owner, view_start, view_length, block_list, positive_offset
):
    d_history, d_w = pl.pallas_call(
        whole_kernel,
        out_shape=(
            jax.ShapeDtypeStruct((SLOTS, ORROWS, D), BF),
            jax.ShapeDtypeStruct((8, WCOLS), F32),
        ),
        in_specs=[SM, VM, VM, VM, VM, HB, HB, HB],
        out_specs=(VM, VM),
        scratch_shapes=[
            vmem(BF, D, 3 * D),
            vmem(BF, D, D),
            vmem(I32, 128, 128),
            vmem(I32, 128, 128),
            pltpu.SMEM((WIDE,), I32),
            vmem(I32, WIDE, 1, 128),
            vmem(I32, WIDE, 1, 128),
            pltpu.SMEM((WIDE, 1, 128), I32),
            pltpu.SMEM((OWNED,), I32),
            pltpu.SMEM((WIDE,), I32),
            vmem(I32, OWNED, 128),
            vmem(BF, SLOTS, QROWS, QCOLS),
            vmem(BF, NARROW, OWNED, QROWS, QCOLS),
            vmem(BF, ROWS, D),
            vmem(BF, D, ROWS),
            vmem(BF, ROWS, 3 * D),
            vmem(BF, ROWS, 2 * D),
            vmem(F32, ROWS, 128),
            vmem(BF, OWNED, SPAN, D),
            vmem(F32, ROWS, D),
            vmem(F32, OWNED, D),
            vmem(F32, OWNED, D),
            vmem(F32, OWNED, D + 128),
            vmem(F32, NARROW, OWNED, D + 128),
            vmem(F32, NARROW * OWNED, D),
            vmem(F32, OWNED, D),
            vmem(F32, OWNED, D),
            vmem(BF, ROWS, 3 * D),
            vmem(F32, ROWS, D),
            vmem(BF, ROWS, D),
            vmem(BF, 4, 16, 2, WROWS, D),
            vmem(BF, 4, 16, WROWS, D),
            vmem(BF, 4, 4, 4, WROWS, D),
            vmem(BF, 4, 4, 4, WROWS, D),
            vmem(BF, 4, 4, WROWS, D),
            vmem(BF, 4, 4, WROWS, D),
            vmem(F32, 4, WROWS + 8, D),
            vmem(F32, 4, NARROW, 8, D),
            vmem(F32, 4, NARROW, 8, D),
            *[vmem(BF, WIDE, nr, nc) for _, nr, _, nc, _ in BOXES],
            *[vmem(BF, WIDE, nr, nc) for _, nr, _, nc, _ in BOXES],
            *[vmem(BF, NARROW, OWNED, ORROWS, nc) for _, nc, _ in BACKS],
            *[vmem(BF, NARROW, OWNED, ORROWS, nc) for _, nc, _ in BACKS],
            *[vmem(BF, 2, OWNED // 2, ORROWS, nc) for _, nc, _ in BACKS],
            *[vmem(BF, OWNED, ORROWS, nc) for _, nc, _ in BACKS],
            *[vmem(BF, WIDE, ORROWS, nc) for _, nc, _ in BACKS],
            *[vmem(BF, WIDE, ORROWS, nc) for _, nc, _ in BACKS],
            DMA((2,)), DMA, DMA, DMA((2,)),
            DMA((NBOX,)), DMA((NBOX,)),
            DMA((NBOX, 4)), DMA((NBOX, 4)),
            DMA((NARROW,)), DMA((NARROW,)),
            DMA((4,)), DMA((4,)),
            DMA((4, 4)), DMA((4, 4)),
            DMA((4, 4)), DMA((4, 4)),
            DMA((4, 4)), DMA((4, 4)),
            DMA((NBACK, 6)), DMA((NBACK, 6)),
            DMA((NBACK,)), DMA((NBACK,)),
        ],
        compiler_params=pltpu.CompilerParams(
            collective_id=0, has_side_effects=True, vmem_limit_bytes=VMEM_LIMIT
        ),
        name="step",
    )(
        dest_owner, view_start.T, view_length.T, positive_offset.T,
        block_list.reshape(SLOTS, 16).T, history, w_qkv, w_out,
    )
    return pl.pallas_call(
        finish_kernel,
        out_shape=(
            jax.ShapeDtypeStruct((SLOTS, ORROWS, D), F32),
            jax.ShapeDtypeStruct((6, 3 * D), F32),
            jax.ShapeDtypeStruct((6, D), F32),
        ),
        in_specs=[VM, VM],
        out_specs=(VM, VM, VM),
        name="finish",
    )(d_history, d_w)


def solution(mesh):
    return jax.shard_map(
        on_device,
        mesh=mesh,
        in_specs=(
            P("wide", None, None),
            P(),
            P(),
            P("wide"),
            P("wide", "narrow"),
            P("wide", "narrow"),
            P("wide", "narrow", None, None),
            P("wide", "narrow"),
        ),
        out_specs=(
            P("wide", "narrow", None),
            P(("wide", "narrow"), None),
            P(("wide", "narrow"), None),
        ),
        check_vma=False,
    )
```
